32 devices in a mesh: dp: 4 (over y, x), seq: 8 (over z, core).
Axes of the slice: x: 2, y: 2, z: 4, core: 2. Of those that a mesh axis runs over, the one named last changes fastest.
Arguments:
- latents: bfloat16 [4, 8, 256, 1152], P('dp', 'seq'), may hold values from -6 to 6
- in_weight: bfloat16 [1152, 3456], replicated
- out_weight: bfloat16 [1152, 1152], replicated, may hold values from -0.1875 to 0.1875
- cotangent: bfloat16 [4, 8, 256, 1152], P('dp', 'seq'), may hold values from -6 to 6
- clip_lengths: int32 [4, 4], P('dp'), may hold values from 1 to 4, 8 in all within a row
Outputs:
- mixed: bfloat16 [4, 8, 256, 1152], P('dp', 'seq')
- grad_latents: bfloat16 [4, 8, 256, 1152], P('dp', 'seq')
- out_grad: float32 [1152, 1152], P('seq')
The draws below stay inside these ranges and needn't reach their ends.
Inputs may be any that keep to these rules, and one draw needn't show every extreme that they name: `clip_lengths`: the 4 lengths of a sequence sum to 8; in every sequence the longest is exactly 4.
All inputs are finite; a program needn't handle non-finite values.
Results may differ from the reference program's by a relative error of at most 0.013.
The reference program's roundings to bfloat16 on the way count: a program that leaves them out, or rounds other values in their place, can miss the bound.
Values may be sent and summed in bfloat16 or wider, within the bound.
No kernel may reach another device: no remote copies, remote signals or barrier semaphores. Data moves between devices by JAX's collectives and lax.ppermute only.
A program may use at most 128 MiB of HBM per device.

```python
import math
import jax
import jax.numpy as jnp
import numpy as np
from jax import lax

D = 1152
HEADS = 16
HD = 72
P_SIZE = 256
CLIPS = 4
FRAMES = 8
MAXCLIP = 4
N_DP = 4


def draw_in_weight(key, part):
    key = jax.random.fold_in(key, 7)
    inner = HEADS * HD
    base = jax.random.normal(key, (D, 3 * inner), jnp.float32) * D ** (-0.5)
    return base.astype(jnp.bfloat16)


def with_spikes(values, rng, source, target, shards_of, factor):
    def block_of(dim):
        return (jnp.arange(values.shape[dim]) // (values.shape[dim] // shards_of)).reshape((-1,) + (1,) * (values.ndim - 1 - dim))

    near = jax.random.permutation(rng, shards_of)[block_of(target)]
    far = (block_of(target) + shards_of // 2) % shards_of
    return jnp.where((block_of(source) == near) | (block_of(source) == far), factor * values, values)


def shard_levels(stream_key, extent, pieces, least, high):
    def one(dim, blocks):
        draws = jax.random.uniform(jax.random.fold_in(jax.random.fold_in(stream_key, 6), dim), (blocks,), jnp.float32, least / len(pieces), high / len(pieces))
        return jnp.repeat(jnp.exp(draws), extent[dim] // blocks).reshape((-1,) + (1,) * (len(extent) - dim - 1))

    loudness = one(*pieces[0])
    for cut in pieces[1:]:
        loudness = loudness * one(*cut)
    return loudness


def length_profile(amount, total, bound, lean):
    weights = [(1 << 20) // math.isqrt(standing ** lean) + 1 for standing in range(2, amount + 1)]
    spare, counts = total - bound - (amount - 1), [1] * (amount - 1)
    while spare > 0:
        free = [i for i in range(amount - 1) if counts[i] < bound]
        whole, left = sum([weights[i] for i in free]), spare
        for i in free:
            extra = min(bound - counts[i], max(1, left * weights[i] // whole), spare)
            counts[i] = counts[i] + extra
            spare = spare - extra
    return np.array([bound] + counts)


def ragged_sizes(own_key, count, total, bound, skew):
    if count == 2:
        one = jax.random.randint(own_key, (), max(1, total - bound), min(bound, total - 1) + 1)
        return jnp.stack([one, total - one])
    sizes = jnp.asarray(length_profile(count, total, bound, skew), jnp.int32)
    pairs = (count - 1) // 2
    source_of, sink = sizes[1:1 + 2 * pairs:2], sizes[2:2 + 2 * pairs:2]
    margin = jnp.minimum(source_of - 1, bound - sink)
    passed = jax.random.randint(jax.random.fold_in(own_key, 1), (pairs,), 0, 1 << 20) % (margin + 1)
    sizes = sizes.at[1:1 + 2 * pairs:2].set(source_of - passed).at[2:2 + 2 * pairs:2].set(sink + passed)
    return sizes[jax.random.permutation(jax.random.fold_in(own_key, 2), count)]


def bell_draw(stream_key, extent, scale, limit, shards=(), held_as=jnp.bfloat16):
    result = scale * jax.random.normal(stream_key, extent, jnp.float32)
    if shards:
        result = result * shard_levels(stream_key, extent, shards, -0.22, 0.18)
    return jnp.clip(result, -limit, limit).astype(held_as)


def gaussian_with(own_key, dims, scale, most, cuts, heavy, kind=jnp.bfloat16):
    values = scale * jax.random.normal(own_key, dims, jnp.float32)
    if cuts:
        values = values * shard_levels(own_key, dims, cuts, -0.22, 0.18)
    return jnp.clip(with_spikes(values, jax.random.fold_in(own_key, 3), *heavy), -most, most).astype(kind)


def setup_inputs(seed: int = 0) -> dict:
    key_of = jax.random.split(jax.random.key(seed), 6)
    return {
        "latents": gaussian_with(key_of[0], (N_DP, FRAMES, P_SIZE, D), 1.0, 6.0, ((0, 4), (1, 8)), (1, 3, 8, 2.0)),
        "in_weight": draw_in_weight(jax.random.fold_in(key_of[5], 71), 0),
        "out_weight": bell_draw(key_of[2], (HEADS * HD, D), (HEADS * HD) ** -0.5, 0.1875),
        "cotangent": bell_draw(key_of[3], (N_DP, FRAMES, P_SIZE, D), 1.0, 6.0, ((0, 4), (1, 8))),
        "clip_lengths": jax.vmap(lambda own: ragged_sizes(own, CLIPS, FRAMES, MAXCLIP, 1))(jax.random.split(key_of[4], N_DP)).reshape((N_DP, CLIPS)).astype(jnp.int32),
    }


def clip_index(lengths, frames):
    ends = jnp.cumsum(lengths).astype(jnp.int32)
    position = jnp.arange(frames, dtype=jnp.int32)
    return lax.optimization_barrier(jnp.sum((ends[None, :] <= position[:, None]).astype(jnp.int32), axis=1))

def one_sequence(latent_seq, cot_seq, lengths, in_weight, out_weight):
    frames, patches, width = latent_seq.shape
    inner = HEADS * HD
    tok_rows = latent_seq.reshape(frames * patches, width)
    projected = jnp.dot(tok_rows, in_weight, preferred_element_type=jnp.float32).astype(jnp.bfloat16)
    split = projected.reshape(frames, patches, 3, HEADS, HD).astype(jnp.float32)
    query, key_rows, value_rows = (split[:, :, 0], split[:, :, 1], split[:, :, 2])
    clip = clip_index(lengths, frames)
    same = clip[:, None] == clip[None, :]
    scale = 1.0 / jnp.sqrt(jnp.float32(HD))
    scores = jnp.einsum('fphd,gphd->phfg', query, key_rows) * scale
    scores = jnp.where(same[None, None], scores, -jnp.inf)
    weights32 = jax.nn.softmax(scores, axis=-1)
    weights = weights32.astype(jnp.bfloat16).astype(jnp.float32)
    attended = jnp.einsum('phfg,gphd->fphd', weights, value_rows).astype(jnp.bfloat16)
    att_rows = attended.reshape(frames * patches, inner)
    mixed = jnp.dot(att_rows, out_weight, preferred_element_type=jnp.float32).astype(jnp.bfloat16)
    cot_rows = cot_seq.reshape(frames * patches, width)
    grad_att = jnp.dot(cot_rows, out_weight.T, preferred_element_type=jnp.float32).astype(jnp.bfloat16)
    out_grad = jnp.dot(att_rows.T, cot_rows, preferred_element_type=jnp.float32)
    grad_heads = grad_att.reshape(frames, patches, HEADS, HD).astype(jnp.float32)
    grad_weights = jnp.einsum('fphd,gphd->phfg', grad_heads, value_rows)
    grad_values = jnp.einsum('phfg,fphd->gphd', weights, grad_heads).astype(jnp.bfloat16)
    totals = lax.optimization_barrier(jnp.sum(weights32 * grad_weights, axis=-1, keepdims=True))
    grad_scores = (weights32 * (grad_weights - totals) * scale).astype(jnp.bfloat16).astype(jnp.float32)
    grad_query = jnp.einsum('phfg,gphd->fphd', grad_scores, key_rows).astype(jnp.bfloat16)
    grad_keys = jnp.einsum('phfg,fphd->gphd', grad_scores, query).astype(jnp.bfloat16)
    grad_proj = jnp.stack([grad_query, grad_keys, grad_values], axis=2).reshape(frames * patches, 3 * inner)
    grad_lat = jnp.dot(grad_proj, in_weight.T, preferred_element_type=jnp.float32).astype(jnp.bfloat16)
    return (mixed.reshape(frames, patches, width), grad_lat.reshape(frames, patches, width), out_grad)

def reference(latents, in_weight, out_weight, cotangent, clip_lengths):

    def step(items):
        return one_sequence(items[0], items[1], items[2], in_weight, out_weight)
    mixed, grad_latents, out_grads = lax.map(step, (latents, cotangent, clip_lengths))
    return (mixed, grad_latents, lax.optimization_barrier(jnp.sum(out_grads, axis=0)))
```

```python
import functools

import jax
import jax.numpy as jnp
import numpy as np
from jax import lax
from jax.experimental import pallas as pl
from jax.experimental.pallas import tpu as pltpu
from jax.sharding import PartitionSpec as P

HEADS = 16
HD = 72


def clip_index(lengths, frames):
    ends = jnp.cumsum(lengths)
    position = jnp.arange(frames, dtype=jnp.int32)
    return jnp.sum((ends[None, :] <= position[:, None]).astype(jnp.int32), axis=1)


def softmax_weights(query, key_rows, same):
    scale = 1.0 / jnp.sqrt(jnp.float32(HD))
    scores = (
        jnp.einsum("fphd,gphd->phfg", query, key_rows, preferred_element_type=jnp.float32) * scale
    )
    scores = jnp.where(same[None, None], scores, -jnp.inf)
    return jax.nn.softmax(scores, axis=-1)


def contract_rows(left, right):
    return lax.dot_general(
        left, right, (((0,), (0,)), ((), ())), preferred_element_type=jnp.float32
    )


def contract_cols(left, right):
    return lax.dot_general(
        left, right, (((1,), (1,)), ((), ())), preferred_element_type=jnp.float32
    )


def swap(value, axis, flip):
    size = lax.axis_size(axis)
    return lax.ppermute(value, axis, [(i, i ^ flip) for i in range(size)])


def reduce_out(part):
    mine = lax.psum_scatter(part, "seq", scatter_dimension=0, tiled=True)
    return lax.psum(mine.astype(jnp.bfloat16), "dp").astype(jnp.float32)


def patch_body(latents, in_weight, out_weight, cotangent, clip_lengths):
    shards = lax.axis_size("seq")
    local_frames = latents.shape[1]
    patches = latents.shape[2]
    width = latents.shape[3]
    frames = local_frames * shards
    local_patches = patches // shards
    inner = HEADS * HD

    def to_patches(rows):
        return lax.all_to_all(rows, "seq", split_axis=2, concat_axis=1, tiled=True)

    def to_frames(rows):
        return lax.all_to_all(rows, "seq", split_axis=1, concat_axis=2, tiled=True)

    lat_rows = to_patches(latents).reshape(frames * local_patches, width)
    cot_rows = to_patches(cotangent).reshape(frames * local_patches, width)
    projected = jnp.dot(lat_rows, in_weight, preferred_element_type=jnp.float32).astype(
        jnp.bfloat16
    )
    split = projected.reshape(frames, local_patches, 3, HEADS, HD)
    query, key_rows, value_rows = (split[:, :, 0], split[:, :, 1], split[:, :, 2])
    clip = clip_index(clip_lengths[0], frames)
    same = clip[:, None] == clip[None, :]
    weights32 = softmax_weights(query, key_rows, same)
    weights = weights32.astype(jnp.bfloat16)
    attended = jnp.einsum(
        "phfg,gphd->fphd", weights, value_rows, preferred_element_type=jnp.float32
    ).astype(jnp.bfloat16)
    att_rows = attended.reshape(frames * local_patches, inner)
    out_grad = reduce_out(contract_rows(att_rows, cot_rows))
    mixed = jnp.dot(att_rows, out_weight, preferred_element_type=jnp.float32).astype(jnp.bfloat16)
    mixed = to_frames(mixed.reshape(1, frames, local_patches, width))
    grad_att = contract_cols(cot_rows, out_weight).astype(jnp.bfloat16)
    grad_heads = grad_att.reshape(frames, local_patches, HEADS, HD)
    grad_weights = jnp.einsum(
        "fphd,gphd->phfg", grad_heads, value_rows, preferred_element_type=jnp.float32
    )
    grad_values = jnp.einsum(
        "phfg,fphd->gphd", weights, grad_heads, preferred_element_type=jnp.float32
    ).astype(jnp.bfloat16)
    totals = jnp.sum(weights32 * grad_weights, axis=-1, keepdims=True)
    scale = 1.0 / jnp.sqrt(jnp.float32(HD))
    grad_scores = (weights32 * (grad_weights - totals) * scale).astype(jnp.bfloat16)
    grad_query = jnp.einsum(
        "phfg,gphd->fphd", grad_scores, key_rows, preferred_element_type=jnp.float32
    ).astype(jnp.bfloat16)
    grad_keys = jnp.einsum(
        "phfg,fphd->gphd", grad_scores, query, preferred_element_type=jnp.float32
    ).astype(jnp.bfloat16)
    grad_proj = jnp.stack([grad_query, grad_keys, grad_values], axis=2)
    grad_rows = grad_proj.reshape(frames * local_patches, 3 * inner)
    grad_latents = contract_cols(grad_rows, in_weight).astype(jnp.bfloat16)
    grad_latents = to_frames(grad_latents.reshape(1, frames, local_patches, width))
    return (mixed.reshape(latents.shape), grad_latents.reshape(latents.shape), out_grad)


ROWS = 64
PAIRS = 16
TILE = 128
INNER = HEADS * HD
PIECE = 40
SMEM = pl.BlockSpec(memory_space=pltpu.SMEM)
VMEM = pl.BlockSpec(memory_space=pltpu.VMEM)
HBM = pl.BlockSpec(memory_space=pltpu.HBM)
CHUNKS = ((0, 256), (256, 256), (512, 256), (768, 256), (1024, 128))


def shaped(shape, dtype=jnp.bfloat16):
    return jax.ShapeDtypeStruct(shape, dtype)


def dot(left, right):
    return jnp.dot(left, right, preferred_element_type=jnp.float32)


def flat(value):
    return value.reshape(value.shape[0] * ROWS, value.shape[2])


def call(kernel, scalars, inputs, outs, scratch=(), limit=8, flops=10**6, to_hbm=False, size=None):
    size = size or sum(x.size * x.dtype.itemsize for x in (*inputs, *outs))
    return pl.pallas_call(
        kernel,
        out_shape=list(outs),
        in_specs=[SMEM] * len(scalars) + [VMEM] * len(inputs),
        out_specs=[HBM if to_hbm else VMEM] * len(outs),
        scratch_shapes=[x if hasattr(x, "memory_space") else pltpu.VMEM(*x) for x in scratch],
        compiler_params=pltpu.CompilerParams(vmem_limit_bytes=limit << 20),
        cost_estimate=pl.CostEstimate(flops=flops, bytes_accessed=size, transcendentals=0),
    )(*scalars, *inputs)


def roles(spot):
    zpos, lens = spot[0] // 2, [spot[2 + i] for i in range(3)]
    first = 2 * zpos
    ends = [lens[0], lens[0] + lens[1], lens[0] + lens[1] + lens[2]]
    long = jnp.where(
        lens[0] == 4, 0, jnp.where(lens[1] == 4, ends[0], jnp.where(lens[2] == 4, ends[1], ends[2]))
    )

    def clip(frame):
        return sum((end <= frame).astype(jnp.int32) for end in ends)

    ids = [
        jnp.where(zpos == 0, -1, clip(first - 1)),
        clip(first),
        clip(first + 1),
        jnp.where(zpos == 3, -2, clip(first + 2)),
    ]
    return {
        "core": spot[0] % 2,
        "odd": zpos % 2,
        "left": 6 - 2 * (zpos % 2),
        "right": 4 + 2 * (zpos % 2),
        "ids": ids,
        "low": long == first,
        "high": long == first - 2,
        "middle": long == first - 1,
        "tail": long == first - 3,
        "head": long == first + 1,
    }


def slots(role, window):
    low, high, left, right = role["low"], role["high"], role["left"], role["right"]
    in_low = ((0, 2, right, right + 1), (1, 3, left, left + 1))[window]
    in_high = ((left, left + 1, 1, 3), (0, 2, right, right + 1))[window]
    usual = (left + window, window, 2 + window, right + window)
    blocks = [
        jnp.where(low, a, jnp.where(high, b, c)) for a, b, c in zip(in_low, in_high, usual)
    ]
    even, middle = low | high, role["middle"]
    odd = [middle, ~even & ~role["tail"], ~even & ~role["head"], middle]
    return blocks, [even | x for x in odd] if window == 0 else odd


def own_kernel(spot, rows, mine):
    for i in range(2):
        mine[i] = rows[2 * (spot[0] % 2) + i]


def pick_kernel(spot, own, sib, near, far, both):
    role = roles(spot)
    core, odd = role["core"], role["odd"]
    for i in range(2):
        both[2 * core + i] = own[i if own.shape[0] == 2 else 2 * core + i]
        both[2 * (1 - core) + i] = sib[2 * core + i]
    right = (jnp.where(role["low"], 1, 2), 3)
    left = (0, jnp.where(role["high"], 2, 1))
    for i in range(2):
        near[i] = both[jnp.where(odd == 1, left[i], right[i])]
        far[i] = both[jnp.where(odd == 1, right[i], left[i])]


def early_kernel(lat_ab, wi_ref, qkv_ref):
    x = flat(lat_ab[...])
    for j in range(3):
        cols = slice(j * INNER, (j + 1) * INNER)
        qkv_ref[:, :, cols] = dot(x, wi_ref[:, cols]).astype(jnp.bfloat16).reshape(4, ROWS, INNER)


def pair(f, g, w=0, count=1):
    start = (4 * f + g) * 2 * ROWS + w * ROWS
    return slice(start, start + count * ROWS)


def lanes(t, offset=0):
    return slice(offset + TILE * t, offset + TILE * (t + 1))


def forward_kernel(
    spot, near, far, wi_ref, ab_ref, heads_ref, qkv_ref, att_ref, p_ref, wide_ref,
    x_scr, hi_scr, w_scr,
):
    x_scr[:2] = near[...]
    x_scr[2:] = far[...]
    qkv_ref[:4] = ab_ref[...]
    x = flat(x_scr[...])
    for j in range(3):
        cols = slice(j * INNER, (j + 1) * INNER)
        qkv_ref[4:, :, cols] = dot(x, wi_ref[:, cols]).astype(jnp.bfloat16).reshape(4, ROWS, INNER)
    role = roles(spot)
    even, ids = role["low"] | role["high"], role["ids"]
    windows = [slots(role, w) for w in range(2)]
    for w, (blocks, _) in enumerate(windows):
        for t in range(INNER // TILE):
            q = [qkv_ref[blocks[f], :, lanes(t)] for f in range(4)]
            k = [qkv_ref[blocks[g], :, lanes(t, INNER)] for g in range(4)]
            for f in range(4):
                for g in range(4):
                    hi_scr[pair(f, g, w), lanes(t)] = q[f] * k[g]
    scores = contract_cols(heads_ref[...], hi_scr[...])
    for f in range(4):
        line = []
        for g in range(4):
            bias = jnp.where(even | (ids[f] == ids[g]), 0.0, -jnp.inf)
            line.append(scores[:, pair(f, g, 0, 2)] * HD**-0.5 + bias)
        top = jnp.maximum(jnp.maximum(line[0], line[1]), jnp.maximum(line[2], line[3]))
        line = [jnp.exp(x - top) for x in line]
        share = 1.0 / (line[0] + line[1] + line[2] + line[3])
        for g in range(4):
            p_ref[:, pair(f, g, 0, 2)] = line[g] * share
    w_scr[...] = p_ref[...].T.astype(jnp.bfloat16)
    for f in range(4):
        rows = pair(f, 0, 0, 8)
        for start, size in CHUNKS:
            cols = slice(start, start + size)
            spread = dot(w_scr[rows, :], heads_ref[:, cols])
            wide_ref[rows, cols] = spread.astype(jnp.bfloat16)
            for w, (blocks, kept) in enumerate(windows):
                base = 2 * INNER + start
                total = sum(
                    spread[pair(0, g, w)] * qkv_ref[blocks[g], :, base : base + size].astype(jnp.float32)
                    for g in range(4)
                )
                total = total * jnp.where(kept[f], 1.0, 0.0)
                att_ref[blocks[f], :, cols] = total.astype(jnp.bfloat16)


def part_rows(core, att_t, cot, rows):
    height = att_t.shape[0] // 8
    for z in range(4):
        start = pl.multiple_of((2 * z + core) * height, 16)
        rows[z * height : (z + 1) * height, :] = att_t[pl.ds(start, height), :]
    return dot(rows[...], flat(cot[...])).reshape(4, height, -1)


def part_kernel(spot, att_ref, ab_ref, near, far, sib_ref, att_t, cot, rows):
    cot[:4] = ab_ref[...]
    cot[4:6] = near[...]
    cot[6:] = far[...]
    att_t[...] = flat(att_ref[...]).T
    sib_ref[...] = part_rows(1 - spot[0] % 2, att_t, cot, rows).astype(jnp.bfloat16)


def mix_kernel(att_ref, w_ref, here_ref, near_ref, far_ref):
    made = dot(flat(att_ref[...]), w_ref[...]).astype(jnp.bfloat16).reshape(8, ROWS, -1)
    here_ref[...] = made[:4]
    near_ref[...] = made[4:6]
    far_ref[...] = made[6:]


def grad_att_kernel(cot, wo_ref, ga_ref):
    made = contract_cols(flat(cot[...]), wo_ref[...])
    ga_ref[...] = made.astype(jnp.bfloat16).reshape(8, ROWS, INNER)


def backward_kernel(
    spot, ga_ref, qkv_ref, p_ref, wide_ref, heads_ref, d_ref, hi_scr, t_scr, s_scr
):
    role = roles(spot)
    windows = [slots(role, w)[0] for w in range(2)]
    for w, blocks in enumerate(windows):
        for t in range(INNER // TILE):
            do = [ga_ref[blocks[f], :, lanes(t)] for f in range(4)]
            v = [qkv_ref[blocks[g], :, lanes(t, 2 * INNER)] for g in range(4)]
            for f in range(4):
                for g in range(4):
                    hi_scr[pair(f, g, w), lanes(t)] = do[f] * v[g]
    grads = contract_cols(heads_ref[...], hi_scr[...])
    for f in range(4):
        p = [p_ref[:, pair(f, g, 0, 2)] for g in range(4)]
        line = [grads[:, pair(f, g, 0, 2)] for g in range(4)]
        total = sum(p[g] * line[g] for g in range(4))
        for g in range(4):
            t_scr[:, pair(f, g, 0, 2)] = p[g] * (line[g] - total) * HD**-0.5
    s_scr[...] = t_scr[...].T.astype(jnp.bfloat16)
    for start, size in CHUNKS:
        cols = slice(start, start + size)
        spread = dot(s_scr[...], heads_ref[:, cols])
        for w, blocks in enumerate(windows):

            def take(ref, block, offset=0):
                return ref[block, :, offset + start : offset + start + size].astype(jnp.float32)

            def put(block, offset, value):
                d_ref[block, :, offset + start : offset + start + size] = value.astype(jnp.bfloat16)

            do = [take(ga_ref, blocks[f]) for f in range(4)]
            for g in range(4):
                put(
                    blocks[g], 2 * INNER,
                    sum(wide_ref[pair(f, g, w), cols].astype(jnp.float32) * do[f] for f in range(4)),
                )
            q = [take(qkv_ref, blocks[f]) for f in range(4)]
            k = [take(qkv_ref, blocks[g], INNER) for g in range(4)]
            for f in range(4):
                put(blocks[f], 0, sum(spread[pair(f, g, w)] * k[g] for g in range(4)))
            for g in range(4):
                put(blocks[g], INNER, sum(spread[pair(f, g, w)] * q[f] for f in range(4)))


def latents_kernel(d_ref, wi_ref, *outs, first):
    tile = 384
    for j in range(wi_ref.shape[0] // tile):
        cols = slice(j * tile, (j + 1) * tile)
        made = contract_cols(flat(d_ref[first : first + 4]), wi_ref[cols, :]).astype(jnp.bfloat16)
        made = made.reshape(4, ROWS, tile)
        size = 4 // len(outs)
        for i, out in enumerate(outs):
            out[:, :, cols] = made[i * size : (i + 1) * size]


def settle_kernel(spot, *refs):
    *given, own, sib, held = refs
    role = roles(spot)
    core, left, right = role["core"], role["left"], role["right"]
    low, high, tail, head = role["low"], role["high"], role["tail"], role["head"]
    where = [
        jnp.where(high | tail, left, 0),
        jnp.where(low, right, jnp.where(tail, left + 1, 1)),
        jnp.where(high, left + 1, jnp.where(head, right, 2)),
        jnp.where(low | head, right + 1, 3),
    ]
    for base in (0, 2):
        here, near, far = given[:3] if base == 0 else given[3:]
        held[:4] = here[...]
        held[4:6] = near[...]
        held[6:] = far[...]
        for i in range(2):
            own[base + i] = held[jnp.where(core == 0, where[i], where[2 + i])]
            sib[base + i] = held[jnp.where(core == 0, where[2 + i], where[i])]


def cut(zpos, group):
    wide_first = jnp.where(group < 2, 40 * group, 32 * group + 16)
    wide_last = jnp.where(group < 2, 32 * group, 40 * group - 16)
    return pl.multiple_of(jnp.where(zpos % 2 == 0, wide_first, wide_last), 8)


def packed(zpos, group):
    first = jnp.where(zpos == 0, 0, jnp.where(zpos == 1, 40, jnp.where(zpos == 2, 72, 112)))
    second = jnp.where(zpos == 0, 0, jnp.where(zpos == 1, 32, jnp.where(zpos == 2, 72, 104)))
    return pl.multiple_of(jnp.where(group < 2, first, second), 8)


def cores_kernel(spot, att_t, cot, got, keep, *sends):
    group = spot[1]
    *sends, rows, total, pack = sends
    height = got.shape[1]
    made = part_rows(spot[0] % 2, att_t, cot, rows)
    for z in range(4):
        total[z * height : (z + 1) * height, :] = made[z] + got[z].astype(jnp.float32)
    for flip, out in enumerate((keep, *sends)):
        whose = group ^ flip
        for z in range(4):
            start = pl.multiple_of(z * height + cut(z, whose), 8)
            pack[pl.ds(packed(z, whose), PIECE), :] = total[pl.ds(start, PIECE), :]
        out[...] = pack[:height, :].astype(out.dtype)


def groups_kernel(spot, own, one, two, three, keep, *sends):
    zpos, group = spot[0] // 2, spot[1]
    *sends, total = sends
    height = own.shape[0]
    total[:height, :] = own[...] + sum(x[...].astype(jnp.float32) for x in (one, two, three))
    total[height:, :] = jnp.zeros((total.shape[0] - height, total.shape[1]), jnp.float32)
    for flip, out in enumerate((keep, *sends)):
        out[...] = total[pl.ds(packed(zpos ^ flip, group), PIECE), :].astype(out.dtype)


def chips_kernel(own, one, two, three, out):
    total = own[...] + sum(x[...].astype(jnp.float32) for x in (one, two, three))
    out[...] = total.astype(jnp.bfloat16)


def gather_kernel(spot, own, one, two, three, out, held, rows):
    zpos, group = spot[0] // 2, spot[1]
    for flip, value in enumerate((own, one, two, three)):
        held[group ^ flip] = value[...].astype(jnp.float32)
    for whose in range(4):
        rows[pl.ds(cut(zpos, whose), PIECE), :] = held[whose]
    out[...] = rows[: out.shape[0], :]


def final_kernel(spot, own, sib, rows, mixed, grad, out, sems):
    core = spot[0] % 2
    here, there = pl.ds(2 * core, 2), pl.ds(2 * (1 - core), 2)
    moves = [(rows, out)]
    for base, made in ((0, mixed), (2, grad)):
        moves.append((own.at[base : base + 2], made.at[here]))
        moves.append((sib.at[base : base + 2], made.at[there]))
    copies = [pltpu.make_async_copy(x, y, sems.at[i]) for i, (x, y) in enumerate(moves)]
    for copy in copies:
        copy.start()
    for copy in copies:
        copy.wait()


def after(later, earlier):
    return lax.optimization_barrier((later, earlier))


def swap_near(value):
    return swap(value, "seq", 2)


def swap_far(value):
    return lax.ppermute(value, "seq", [(2, 4), (4, 2), (3, 5), (5, 3)])


def clip_body(latents, in_weight, out_weight, cotangent, clip_lengths):
    width = latents.shape[3]
    rows = INNER // 8
    wide = jnp.float32
    place = jnp.arange(2 + clip_lengths.shape[1], dtype=jnp.int32)
    spot = jnp.where(place == 0, lax.axis_index("seq"), jnp.where(place == 1, lax.axis_index("dp"), 0))
    spot = spot + jnp.pad(clip_lengths[0], (2, 0))
    heads = jnp.asarray(np.arange(INNER) // HD == np.arange(HEADS)[:, None], jnp.bfloat16)
    lat = latents.reshape(4, ROWS, width)
    cot = cotangent.reshape(4, ROWS, width)

    bf16 = jnp.bfloat16
    four, two, eight = shaped((4, ROWS, width)), shaped((2, ROWS, width)), shaped((8, ROWS, INNER))

    def pick(own, sib):
        near, far, both = call(pick_kernel, [spot], [own, sib], [two, two, four], flops=4 * 10**9)
        return swap_near(near), swap_far(far), both

    lat_sib, cot_sib = swap(lat, "seq", 1), swap(cot, "seq", 1)
    (lat_own,) = call(own_kernel, [spot], [lat], [two], flops=4 * 10**9)
    lat_near, lat_far, lat_ab = pick(lat_own, lat_sib)
    cot, lat_ab = after(cot, lat_ab)
    cot_near, cot_far, cot_ab = pick(cot, cot_sib)
    (qkv_ab,) = call(
        early_kernel, [], [lat_ab, in_weight], [shaped((4, ROWS, 3 * INNER))], limit=16, flops=27 * 10**8
    )
    pairs = 2 * PAIRS * ROWS
    products, columns = ((pairs, INNER), bf16), ((pairs, HEADS), bf16)
    qkv, att, probs, wides = call(
        forward_kernel, [spot], [lat_near, lat_far, in_weight, qkv_ab, heads],
        [shaped((8, ROWS, 3 * INNER)), eight, shaped((HEADS, pairs), wide), shaped((pairs, INNER))],
        [((4, ROWS, width), bf16), products, columns], limit=24, flops=8 * 10**9,
    )
    part_scr = ((4 * rows, 8 * ROWS), bf16)
    other, att_t, cot_all = call(
        part_kernel, [spot], [att, cot_ab, cot_near, cot_far],
        [shaped((4, rows, width)), shaped((INNER, 8 * ROWS)), eight], [part_scr],
        limit=16, flops=7 * 10**8,
    )
    got = swap(other, "seq", 1)
    cot_all, other = after(cot_all, other)
    (ga,) = call(grad_att_kernel, [], [cot_all, out_weight], [eight], limit=16, flops=14 * 10**8)
    att_t, ga = after(att_t, ga)
    part, piece = (rows, width), (PIECE, width)
    keep, *sends = call(
        cores_kernel, [spot], [att_t, cot_all, got], [shaped(part, wide)] + [shaped(part)] * 3,
        [part_scr, ((4 * rows, width), wide), ((rows + 8, width), wide)], limit=16, flops=7 * 10**8,
    )
    att, sends = after(att, sends)
    sends = [swap(x, "dp", flip) for flip, x in enumerate(sends, 1)]
    mixed = call(mix_kernel, [], [att, out_weight], [four, two, two], limit=16, size=10**3)
    qkv, mixed = after(qkv, mixed)
    mixed = [mixed[0], swap_near(mixed[1]), swap_far(mixed[2])]
    (d_all,) = call(
        backward_kernel, [spot], [ga, qkv, probs, wides, heads], [shaped((8, ROWS, 3 * INNER))],
        [products, ((HEADS, pairs), wide), columns], limit=24, size=10**3,
    )
    theirs = functools.partial(latents_kernel, first=4)
    grad = call(theirs, [], [d_all, in_weight], [two, two], limit=16, size=10**3)
    keep, (grad, mixed) = after(keep, (grad, mixed))
    keep, *sends = call(
        groups_kernel, [spot], [keep, *sends], [shaped(piece, wide)] + [shaped(piece)] * 3,
        [((rows + 8, width), wide)],
    )
    sends = [swap(x, "seq", 2 * flip) for flip, x in enumerate(sends, 1)]
    grad, sends[0] = after(grad, sends[0])
    d_all, grad = after(d_all, grad)
    ours = functools.partial(latents_kernel, first=0)
    (own,) = call(ours, [], [d_all, in_weight], [four], limit=16, flops=8 * 10**9)
    grad = [own, swap_near(grad[0]), swap_far(grad[1])]
    keep, grad[0] = after(keep, grad[0])
    (last,) = call(chips_kernel, [], [keep, *sends], [shaped(piece)])
    grad[0], last = after(grad[0], last)
    others = [swap(last, "dp", flip) for flip in (1, 2, 3)]
    own, sib = call(settle_kernel, [spot], [*mixed, *grad], [four, four], [((8, ROWS, width), bf16)])
    (out_grad,) = call(
        gather_kernel, [spot], [last, *others], [shaped(part, wide)],
        [((4, *piece), wide), ((rows + 8, width), wide)], flops=8 * 10**9,
    )
    mixed, grad, out_grad = call(
        final_kernel, [spot], [own, swap(sib, "seq", 1), out_grad],
        [four, four, shaped((rows, width), wide)], [pltpu.SemaphoreType.DMA((5,))], to_hbm=True,
    )
    return mixed.reshape(latents.shape), grad.reshape(latents.shape), out_grad


def body(latents, *others):
    frames, patches = latents.shape[1] * lax.axis_size("seq"), latents.shape[2]
    small = (lax.axis_size("dp"), lax.axis_size("seq"), frames, patches) == (4, 8, 8, 4 * ROWS)
    return (clip_body if small else patch_body)(latents, *others)


def solution(mesh):
    placed = (P("dp", "seq", None, None), P(), P(), P("dp", "seq", None, None), P("dp", None))
    return jax.shard_map(
        body,
        mesh=mesh,
        in_specs=placed,
        out_specs=(P("dp", "seq", None, None), P("dp", "seq", None, None), P("seq", None)),
        check_vma=False,
    )
```

```python
import functools

import jax
import jax.numpy as jnp
import numpy as np
from jax import lax
from jax.experimental import pallas as pl
from jax.experimental.pallas import tpu as pltpu
from jax.sharding import PartitionSpec as P

HEADS = 16
HD = 72


def clip_index(lengths, frames):
    ends = jnp.cumsum(lengths)
    position = jnp.arange(frames, dtype=jnp.int32)
    return jnp.sum((ends[None, :] <= position[:, None]).astype(jnp.int32), axis=1)


def softmax_weights(query, key_rows, same):
    scale = 1.0 / jnp.sqrt(jnp.float32(HD))
    scores = (
        jnp.einsum("fphd,gphd->phfg", query, key_rows, preferred_element_type=jnp.float32) * scale
    )
    scores = jnp.where(same[None, None], scores, -jnp.inf)
    return jax.nn.softmax(scores, axis=-1)


def contract_rows(left, right):
    return lax.dot_general(
        left, right, (((0,), (0,)), ((), ())), preferred_element_type=jnp.float32
    )


def contract_cols(left, right):
    return lax.dot_general(
        left, right, (((1,), (1,)), ((), ())), preferred_element_type=jnp.float32
    )


def swap(value, axis, flip):
    size = lax.axis_size(axis)
    return lax.ppermute(value, axis, [(i, i ^ flip) for i in range(size)])


def reduce_out(part):
    mine = lax.psum_scatter(part, "seq", scatter_dimension=0, tiled=True)
    return lax.psum(mine.astype(jnp.bfloat16), "dp").astype(jnp.float32)


def patch_body(latents, in_weight, out_weight, cotangent, clip_lengths):
    shards = lax.axis_size("seq")
    local_frames = latents.shape[1]
    patches = latents.shape[2]
    width = latents.shape[3]
    frames = local_frames * shards
    local_patches = patches // shards
    inner = HEADS * HD

    def to_patches(rows):
        return lax.all_to_all(rows, "seq", split_axis=2, concat_axis=1, tiled=True)

    def to_frames(rows):
        return lax.all_to_all(rows, "seq", split_axis=1, concat_axis=2, tiled=True)

    lat_rows = to_patches(latents).reshape(frames * local_patches, width)
    cot_rows = to_patches(cotangent).reshape(frames * local_patches, width)
    projected = jnp.dot(lat_rows, in_weight, preferred_element_type=jnp.float32).astype(
        jnp.bfloat16
    )
    split = projected.reshape(frames, local_patches, 3, HEADS, HD)
    query, key_rows, value_rows = (split[:, :, 0], split[:, :, 1], split[:, :, 2])
    clip = clip_index(clip_lengths[0], frames)
    same = clip[:, None] == clip[None, :]
    weights32 = softmax_weights(query, key_rows, same)
    weights = weights32.astype(jnp.bfloat16)
    attended = jnp.einsum(
        "phfg,gphd->fphd", weights, value_rows, preferred_element_type=jnp.float32
    ).astype(jnp.bfloat16)
    att_rows = attended.reshape(frames * local_patches, inner)
    out_grad = reduce_out(contract_rows(att_rows, cot_rows))
    mixed = jnp.dot(att_rows, out_weight, preferred_element_type=jnp.float32).astype(jnp.bfloat16)
    mixed = to_frames(mixed.reshape(1, frames, local_patches, width))
    grad_att = contract_cols(cot_rows, out_weight).astype(jnp.bfloat16)
    grad_heads = grad_att.reshape(frames, local_patches, HEADS, HD)
    grad_weights = jnp.einsum(
        "fphd,gphd->phfg", grad_heads, value_rows, preferred_element_type=jnp.float32
    )
    grad_values = jnp.einsum(
        "phfg,fphd->gphd", weights, grad_heads, preferred_element_type=jnp.float32
    ).astype(jnp.bfloat16)
    totals = jnp.sum(weights32 * grad_weights, axis=-1, keepdims=True)
    scale = 1.0 / jnp.sqrt(jnp.float32(HD))
    grad_scores = (weights32 * (grad_weights - totals) * scale).astype(jnp.bfloat16)
    grad_query = jnp.einsum(
        "phfg,gphd->fphd", grad_scores, key_rows, preferred_element_type=jnp.float32
    ).astype(jnp.bfloat16)
    grad_keys = jnp.einsum(
        "phfg,fphd->gphd", grad_scores, query, preferred_element_type=jnp.float32
    ).astype(jnp.bfloat16)
    grad_proj = jnp.stack([grad_query, grad_keys, grad_values], axis=2)
    grad_rows = grad_proj.reshape(frames * local_patches, 3 * inner)
    grad_latents = contract_cols(grad_rows, in_weight).astype(jnp.bfloat16)
    grad_latents = to_frames(grad_latents.reshape(1, frames, local_patches, width))
    return (mixed.reshape(latents.shape), grad_latents.reshape(latents.shape), out_grad)


ROWS = 64
PAIRS = 16
TILE = 128
INNER = HEADS * HD
PIECE = 41 * 8
SMEM = pl.BlockSpec(memory_space=pltpu.SMEM)
VMEM = pl.BlockSpec(memory_space=pltpu.VMEM)
HBM = pl.BlockSpec(memory_space=pltpu.HBM)
CHUNKS = ((0, 256), (256, 256), (512, 256), (768, 256), (1024, 128))


def shaped(shape, dtype=jnp.bfloat16):
    return jax.ShapeDtypeStruct(shape, dtype)


def dot(left, right):
    return jnp.dot(left, right, preferred_element_type=jnp.float32)


def flat(value):
    return value.reshape(value.shape[0] * ROWS, value.shape[2])


def call(kernel, scalars, inputs, outs, scratch=(), limit=8, flops=10**6, to_hbm=False, size=None, same=None):
    size = size or sum(x.size * x.dtype.itemsize for x in (*inputs, *outs))
    return pl.pallas_call(
        kernel,
        out_shape=list(outs),
        in_specs=[SMEM] * len(scalars) + [VMEM] * len(inputs),
        out_specs=[HBM if to_hbm else VMEM] * len(outs),
        scratch_shapes=[x if hasattr(x, "memory_space") else pltpu.VMEM(*x) for x in scratch],
        input_output_aliases={len(scalars) + same[0]: same[1]} if same else {},
        compiler_params=pltpu.CompilerParams(vmem_limit_bytes=limit << 20),
        cost_estimate=pl.CostEstimate(flops=flops, bytes_accessed=size, transcendentals=0),
    )(*scalars, *inputs)


def roles(spot):
    zpos, lens = spot[0] // 2, [spot[2 + i] for i in range(3)]
    first = 2 * zpos
    ends = [lens[0], lens[0] + lens[1], lens[0] + lens[1] + lens[2]]
    long = jnp.where(
        lens[0] == 4, 0, jnp.where(lens[1] == 4, ends[0], jnp.where(lens[2] == 4, ends[1], ends[2]))
    )

    def clip(frame):
        return sum((end <= frame).astype(jnp.int32) for end in ends)

    ids = [
        jnp.where(zpos == 0, -1, clip(first - 1)),
        clip(first),
        clip(first + 1),
        jnp.where(zpos == 3, -2, clip(first + 2)),
    ]
    return {
        "core": spot[0] % 2,
        "odd": zpos % 2,
        "left": 6 - 2 * (zpos % 2),
        "right": 4 + 2 * (zpos % 2),
        "ids": ids,
        "low": long == first,
        "high": long == first - 2,
        "middle": long == first - 1,
        "tail": long == first - 3,
        "head": long == first + 1,
    }


def slots(role, window):
    low, high, left, right = role["low"], role["high"], role["left"], role["right"]
    in_low = ((0, 2, right, right + 1), (1, 3, left, left + 1))[window]
    in_high = ((left, left + 1, 1, 3), (0, 2, right, right + 1))[window]
    usual = (left + window, window, 2 + window, right + window)
    blocks = [
        jnp.where(low, a, jnp.where(high, b, c)) for a, b, c in zip(in_low, in_high, usual)
    ]
    even, middle = low | high, role["middle"]
    odd = [middle, ~even & ~role["tail"], ~even & ~role["head"], middle]
    return blocks, [even | x for x in odd] if window == 0 else odd


def pick_kernel(spot, own, sib, near, far, both):
    role = roles(spot)
    core, odd = role["core"], role["odd"]
    for i in range(2):
        both[2 * core + i] = own[i if own.shape[0] == 2 else 2 * core + i]
        both[2 * (1 - core) + i] = sib[2 * core + i]
    right = (jnp.where(role["low"], 1, 2), 3)
    left = (0, jnp.where(role["high"], 2, 1))
    for i in range(2):
        near[i] = both[jnp.where(odd == 1, left[i], right[i])]
        far[i] = both[jnp.where(odd == 1, right[i], left[i])]


def early_kernel(lat_ab, wi_ref, qkv_ref):
    x = flat(lat_ab[...])
    for j in range(3):
        cols = slice(j * INNER, (j + 1) * INNER)
        qkv_ref[:4, :, cols] = dot(x, wi_ref[:, cols]).astype(jnp.bfloat16).reshape(4, ROWS, INNER)


def pair(f, g, w=0, count=1):
    start = (4 * f + g) * 2 * ROWS + w * ROWS
    return slice(start, start + count * ROWS)


def lanes(t, offset=0):
    return slice(offset + TILE * t, offset + TILE * (t + 1))


def forward_kernel(
    spot, near, far, wi_ref, _, heads_ref, qkv_ref, att_ref, p_ref, wide_ref,
    x_scr, hi_scr, w_scr,
):
    x_scr[:2] = near[...]
    x_scr[2:] = far[...]
    x = flat(x_scr[...])
    for j in range(3):
        cols = slice(j * INNER, (j + 1) * INNER)
        qkv_ref[4:, :, cols] = dot(x, wi_ref[:, cols]).astype(jnp.bfloat16).reshape(4, ROWS, INNER)
    role = roles(spot)
    even, ids = role["low"] | role["high"], role["ids"]
    windows = [slots(role, w) for w in range(2)]
    for w, (blocks, _) in enumerate(windows):
        for t in range(INNER // TILE):
            q = [qkv_ref[blocks[f], :, lanes(t)] for f in range(4)]
            k = [qkv_ref[blocks[g], :, lanes(t, INNER)] for g in range(4)]
            for f in range(4):
                for g in range(4):
                    hi_scr[pair(f, g, w), lanes(t)] = q[f] * k[g]
    scores = contract_cols(heads_ref[...], hi_scr[...])
    for f in range(4):
        line = []
        for g in range(4):
            bias = jnp.where(even | (ids[f] == ids[g]), 0.0, -jnp.inf)
            line.append(scores[:, pair(f, g, 0, 2)] * HD**-0.5 + bias)
        top = jnp.maximum(jnp.maximum(line[0], line[1]), jnp.maximum(line[2], line[3]))
        line = [jnp.exp(x - top) for x in line]
        share = 1.0 / (line[0] + line[1] + line[2] + line[3])
        for g in range(4):
            p_ref[:, pair(f, g, 0, 2)] = line[g] * share
    w_scr[...] = p_ref[...].T.astype(jnp.bfloat16)
    for f in range(4):
        rows = pair(f, 0, 0, 8)
        for start, size in CHUNKS:
            cols = slice(start, start + size)
            spread = dot(w_scr[rows, :], heads_ref[:, cols])
            wide_ref[rows, cols] = spread.astype(jnp.bfloat16)
            for w, (blocks, kept) in enumerate(windows):
                base = 2 * INNER + start
                total = sum(
                    spread[pair(0, g, w)] * qkv_ref[blocks[g], :, base : base + size].astype(jnp.float32)
                    for g in range(4)
                )
                total = total * jnp.where(kept[f], 1.0, 0.0)
                att_ref[blocks[f], :, cols] = total.astype(jnp.bfloat16)


def part_rows(core, att_t, cot, rows):
    height = att_t.shape[0] // 8
    for z in range(4):
        start = pl.multiple_of((2 * z + core) * height, 16)
        rows[z * height : (z + 1) * height, :] = att_t[pl.ds(start, height), :]
    return dot(rows[...], flat(cot[...])).reshape(4, height, -1)


def part_kernel(spot, att_ref, ab_ref, near, far, sib_ref, att_t, cot, rows):
    cot[:4] = ab_ref[...]
    cot[4:6] = near[...]
    cot[6:] = far[...]
    att_t[...] = flat(att_ref[...]).T
    sib_ref[...] = part_rows(1 - spot[0] % 2, att_t, cot, rows).astype(jnp.bfloat16)


def mix_kernel(att_ref, w_ref, here_ref, near_ref, far_ref):
    made = dot(flat(att_ref[...]), w_ref[...]).astype(jnp.bfloat16).reshape(8, ROWS, -1)
    here_ref[...] = made[:4]
    near_ref[...] = made[4:6]
    far_ref[...] = made[6:]


def grad_att_kernel(cot, wo_ref, ga_ref):
    made = contract_cols(flat(cot[...]), wo_ref[...])
    ga_ref[...] = made.astype(jnp.bfloat16).reshape(8, ROWS, INNER)


def backward_kernel(
    spot, ga_ref, qkv_ref, p_ref, wide_ref, heads_ref, d_ref, hi_scr, t_scr, s_scr
):
    role = roles(spot)
    windows = [slots(role, w)[0] for w in range(2)]
    for w, blocks in enumerate(windows):
        for t in range(INNER // TILE):
            do = [ga_ref[blocks[f], :, lanes(t)] for f in range(4)]
            v = [qkv_ref[blocks[g], :, lanes(t, 2 * INNER)] for g in range(4)]
            for f in range(4):
                for g in range(4):
                    hi_scr[pair(f, g, w), lanes(t)] = do[f] * v[g]
    grads = contract_cols(heads_ref[...], hi_scr[...])
    for f in range(4):
        p = [p_ref[:, pair(f, g, 0, 2)] for g in range(4)]
        line = [grads[:, pair(f, g, 0, 2)] for g in range(4)]
        total = sum(p[g] * line[g] for g in range(4))
        for g in range(4):
            t_scr[:, pair(f, g, 0, 2)] = p[g] * (line[g] - total) * HD**-0.5
    s_scr[...] = t_scr[...].T.astype(jnp.bfloat16)
    for start, size in CHUNKS:
        cols = slice(start, start + size)
        spread = dot(s_scr[...], heads_ref[:, cols])
        for w, blocks in enumerate(windows):

            def take(ref, block, offset=0):
                return ref[block, :, offset + start : offset + start + size].astype(jnp.float32)

            def put(block, offset, value):
                d_ref[block, :, offset + start : offset + start + size] = value.astype(jnp.bfloat16)

            do = [take(ga_ref, blocks[f]) for f in range(4)]
            for g in range(4):
                put(
                    blocks[g], 2 * INNER,
                    sum(wide_ref[pair(f, g, w), cols].astype(jnp.float32) * do[f] for f in range(4)),
                )
            q = [take(qkv_ref, blocks[f]) for f in range(4)]
            k = [take(qkv_ref, blocks[g], INNER) for g in range(4)]
            for f in range(4):
                put(blocks[f], 0, sum(spread[pair(f, g, w)] * k[g] for g in range(4)))
            for g in range(4):
                put(blocks[g], INNER, sum(spread[pair(f, g, w)] * q[f] for f in range(4)))


def latents_kernel(d_ref, wi_ref, *outs, first):
    tile = 384
    for j in range(wi_ref.shape[0] // tile):
        cols = slice(j * tile, (j + 1) * tile)
        made = contract_cols(flat(d_ref[first : first + 4]), wi_ref[cols, :]).astype(jnp.bfloat16)
        made = made.reshape(4, ROWS, tile)
        size = 4 // len(outs)
        for i, out in enumerate(outs):
            out[:, :, cols] = made[i * size : (i + 1) * size]


def settle_kernel(spot, *refs):
    *given, own, sib, held = refs
    role = roles(spot)
    core, left, right = role["core"], role["left"], role["right"]
    low, high, tail, head = role["low"], role["high"], role["tail"], role["head"]
    where = [
        jnp.where(high | tail, left, 0),
        jnp.where(low, right, jnp.where(tail, left + 1, 1)),
        jnp.where(high, left + 1, jnp.where(head, right, 2)),
        jnp.where(low | head, right + 1, 3),
    ]
    for base in (0, 2):
        here, near, far = given[:3] if base == 0 else given[3:]
        held[:4] = here[...]
        held[4:6] = near[...]
        held[6:] = far[...]
        for i in range(2):
            own[base + i] = held[jnp.where(core == 0, where[i], where[2 + i])]
            sib[base + i] = held[jnp.where(core == 0, where[2 + i], where[i])]


def first_row(group, block):
    return pl.multiple_of((group * 81 // 2 + block * 162) * 8, 8)


def cores_kernel(spot, att_t, cot, got, keep, *sends):
    group = spot[1]
    *sends, rows, total = sends
    height, width = got.shape[1:]
    made = part_rows(spot[0] % 2, att_t, cot, rows)
    for z in range(4):
        block = made[z] + got[z].astype(jnp.float32)
        for t in range(width // TILE):
            start = (z * width // TILE + t) * height
            total[start : start + height, :] = block[:, lanes(t)]
    for flip, out in enumerate((keep, *sends)):
        for z in range(4):
            out[z] = total[pl.ds(first_row(group ^ flip, z), PIECE), :].astype(out.dtype)


def groups_kernel(spot, own, one, two, three, keep, *sends):
    zpos = spot[0] // 2
    *sends, total = sends
    total[...] = own[...] + sum(x[...].astype(jnp.float32) for x in (one, two, three))
    for flip, out in enumerate((keep, *sends)):
        out[...] = total[zpos ^ flip].astype(out.dtype)


def chips_kernel(own, one, two, three, out):
    total = own[...] + sum(x[...].astype(jnp.float32) for x in (one, two, three))
    out[...] = total.astype(jnp.bfloat16)


def gather_kernel(spot, own, one, two, three, out, held, rows):
    for flip, value in enumerate((own, one, two, three)):
        held[spot[1] ^ flip] = value[...].astype(jnp.float32)
    for group in range(4):
        rows[pl.ds(first_row(group, 0), PIECE), :] = held[group]
    height, width = out.shape
    for t in range(width // TILE):
        out[:, lanes(t)] = rows[t * height : (t + 1) * height, :]


def final_kernel(spot, own, sib, rows, mixed, grad, out, sems):
    core = spot[0] % 2
    here, there = pl.ds(2 * core, 2), pl.ds(2 * (1 - core), 2)
    moves = [(rows.at[i : i + 48], out.at[i : i + 48]) for i in range(0, out.shape[0], 48)]
    for base, made in ((0, mixed), (2, grad)):
        moves.append((own.at[base : base + 2], made.at[here]))
        moves.append((sib.at[base : base + 2], made.at[there]))
    copies = [pltpu.make_async_copy(x, y, sems.at[i]) for i, (x, y) in enumerate(moves)]
    for copy in copies:
        copy.start()
    for copy in copies:
        copy.wait()


def after(later, earlier):
    return lax.optimization_barrier((later, earlier))


def swap_near(value):
    return swap(value, "seq", 2)


def swap_far(value):
    return lax.ppermute(
        value, "seq", [(0, 0), (1, 1), (2, 4), (4, 2), (3, 5), (5, 3), (6, 6), (7, 7)]
    )


def clip_body(latents, in_weight, out_weight, cotangent, clip_lengths):
    width = latents.shape[3]
    rows = INNER // 8
    wide = jnp.float32
    place = jnp.arange(2 + clip_lengths.shape[1], dtype=jnp.int32)
    spot = jnp.where(place == 0, lax.axis_index("seq"), jnp.where(place == 1, lax.axis_index("dp"), 0))
    spot = spot + jnp.pad(clip_lengths[0], (2, 0))
    heads = jnp.asarray(np.arange(INNER) // HD == np.arange(HEADS)[:, None], jnp.bfloat16)
    lat = latents.reshape(4, ROWS, width)
    cot = cotangent.reshape(4, ROWS, width)

    bf16 = jnp.bfloat16
    four, two, eight = shaped((4, ROWS, width)), shaped((2, ROWS, width)), shaped((8, ROWS, INNER))

    def pick(own, sib):
        near, far, both = call(pick_kernel, [spot], [own, sib], [two, two, four], flops=4 * 10**9)
        return swap_near(near), swap_far(far), both

    lat_sib, cot_sib = swap(lat, "seq", 1), swap(cot, "seq", 1)
    lat_own = lax.dynamic_slice_in_dim(lat, 2 * (lax.axis_index("seq") % 2), 2, 0)
    lat_near, lat_far, lat_ab = pick(lat_own, lat_sib)
    (qkv_ab,) = call(
        early_kernel, [], [lat_ab, in_weight], [shaped((8, ROWS, 3 * INNER))], limit=16, flops=27 * 10**8
    )
    cot_sib, qkv_ab = after(cot_sib, qkv_ab)
    cot_near, cot_far, cot_ab = pick(cot, cot_sib)
    pairs = 2 * PAIRS * ROWS
    products, columns = ((pairs, INNER), bf16), ((pairs, HEADS), bf16)
    qkv, att, probs, wides = call(
        forward_kernel, [spot], [lat_near, lat_far, in_weight, qkv_ab, heads],
        [shaped((8, ROWS, 3 * INNER)), eight, shaped((HEADS, pairs), wide), shaped((pairs, INNER))],
        [((4, ROWS, width), bf16), products, columns], limit=24, flops=8 * 10**9, same=(3, 0),
    )
    part_scr = ((4 * rows, 8 * ROWS), bf16)
    other, att_t, cot_all = call(
        part_kernel, [spot], [att, cot_ab, cot_near, cot_far],
        [shaped((4, rows, width)), shaped((INNER, 8 * ROWS)), eight], [part_scr],
        limit=16, flops=7 * 10**8,
    )
    got = swap(other, "seq", 1)
    cot_all, other = after(cot_all, other)
    (ga,) = call(grad_att_kernel, [], [cot_all, out_weight], [eight], limit=16, flops=14 * 10**8)
    att_t, ga = after(att_t, ga)
    part, piece = (4, PIECE, TILE), (PIECE, TILE)
    tiles = rows * width // TILE
    keep, *sends = call(
        cores_kernel, [spot], [att_t, cot_all, got], [shaped(part, wide)] + [shaped(part)] * 3,
        [part_scr, ((4 * tiles, TILE), wide)], limit=16, flops=7 * 10**8,
    )
    att, sends = after(att, sends)
    sends = [swap(x, "dp", flip) for flip, x in enumerate(sends, 1)]
    mixed = call(mix_kernel, [], [att, out_weight], [four, two, two], limit=16, size=10**3)
    qkv, mixed = after(qkv, mixed)
    mixed = [mixed[0], swap_near(mixed[1]), swap_far(mixed[2])]
    (d_all,) = call(
        backward_kernel, [spot], [ga, qkv, probs, wides, heads], [shaped((8, ROWS, 3 * INNER))],
        [products, ((HEADS, pairs), wide), columns], limit=24, size=10**3,
    )
    theirs = functools.partial(latents_kernel, first=4)
    grad = call(theirs, [], [d_all, in_weight], [two, two], limit=16, size=10**3)
    keep, (grad, mixed) = after(keep, (grad, mixed))
    keep, *sends = call(
        groups_kernel, [spot], [keep, *sends], [shaped(piece, wide)] + [shaped(piece)] * 3,
        [(part, wide)],
    )
    grad, keep = after(grad, keep)
    sends = [swap(x, "seq", 2 * flip) for flip, x in enumerate(sends, 1)]
    d_all, grad = after(d_all, grad)
    ours = functools.partial(latents_kernel, first=0)
    (own,) = call(ours, [], [d_all, in_weight], [four], limit=16, flops=8 * 10**9)
    grad = [own, swap_near(grad[0]), swap_far(grad[1])]
    keep, grad[0] = after(keep, grad[0])
    (last,) = call(chips_kernel, [], [keep, *sends], [shaped(piece)])
    grad[0], last = after(grad[0], last)
    others = [swap(last, "dp", flip) for flip in (1, 2, 3)]
    own, sib = call(settle_kernel, [spot], [*mixed, *grad], [four, four], [((8, ROWS, width), bf16)])
    (out_grad,) = call(
        gather_kernel, [spot], [last, *others], [shaped((rows, width), wide)],
        [(part, wide), ((tiles, TILE), wide)], flops=8 * 10**9,
    )
    mixed, grad, out_grad = call(
        final_kernel, [spot], [own, swap(sib, "seq", 1), out_grad],
        [four, four, shaped((rows, width), wide)], [pltpu.SemaphoreType.DMA((7,))], to_hbm=True,
    )
    return mixed.reshape(latents.shape), grad.reshape(latents.shape), out_grad


def body(latents, *others):
    frames, patches = latents.shape[1] * lax.axis_size("seq"), latents.shape[2]
    small = (lax.axis_size("dp"), lax.axis_size("seq"), frames, patches) == (4, 8, 8, 4 * ROWS)
    return (clip_body if small else patch_body)(latents, *others)


def solution(mesh):
    placed = (P("dp", "seq", None, None), P(), P(), P("dp", "seq", None, None), P("dp", None))
    return jax.shard_map(
        body,
        mesh=mesh,
        in_specs=placed,
        out_specs=(P("dp", "seq", None, None), P("dp", "seq", None, None), P("seq", None)),
        check_vma=False,
    )
```

```python
import functools

import jax
import jax.numpy as jnp
import numpy as np
from jax import lax
from jax.experimental import pallas as pl
from jax.experimental.pallas import tpu as pltpu
from jax.sharding import PartitionSpec as P

HEADS = 16
HD = 72


def clip_index(lengths, frames):
    ends = jnp.cumsum(lengths)
    position = jnp.arange(frames, dtype=jnp.int32)
    return jnp.sum((ends[None, :] <= position[:, None]).astype(jnp.int32), axis=1)


def softmax_weights(query, key_rows, same):
    scale = 1.0 / jnp.sqrt(jnp.float32(HD))
    scores = (
        jnp.einsum("fphd,gphd->phfg", query, key_rows, preferred_element_type=jnp.float32) * scale
    )
    scores = jnp.where(same[None, None], scores, -jnp.inf)
    return jax.nn.softmax(scores, axis=-1)


def contract_rows(left, right):
    return lax.dot_general(
        left, right, (((0,), (0,)), ((), ())), preferred_element_type=jnp.float32
    )


def contract_cols(left, right):
    return lax.dot_general(
        left, right, (((1,), (1,)), ((), ())), preferred_element_type=jnp.float32
    )


def swap(value, axis, flip):
    size = lax.axis_size(axis)
    return lax.ppermute(value, axis, [(i, i ^ flip) for i in range(size)])


def reduce_out(part):
    mine = lax.psum_scatter(part, "seq", scatter_dimension=0, tiled=True)
    return lax.psum(mine.astype(jnp.bfloat16), "dp").astype(jnp.float32)


def patch_body(latents, in_weight, out_weight, cotangent, clip_lengths):
    shards = lax.axis_size("seq")
    local_frames = latents.shape[1]
    patches = latents.shape[2]
    width = latents.shape[3]
    frames = local_frames * shards
    local_patches = patches // shards
    inner = HEADS * HD

    def to_patches(rows):
        return lax.all_to_all(rows, "seq", split_axis=2, concat_axis=1, tiled=True)

    def to_frames(rows):
        return lax.all_to_all(rows, "seq", split_axis=1, concat_axis=2, tiled=True)

    lat_rows = to_patches(latents).reshape(frames * local_patches, width)
    cot_rows = to_patches(cotangent).reshape(frames * local_patches, width)
    projected = jnp.dot(lat_rows, in_weight, preferred_element_type=jnp.float32).astype(
        jnp.bfloat16
    )
    split = projected.reshape(frames, local_patches, 3, HEADS, HD)
    query, key_rows, value_rows = (split[:, :, 0], split[:, :, 1], split[:, :, 2])
    clip = clip_index(clip_lengths[0], frames)
    same = clip[:, None] == clip[None, :]
    weights32 = softmax_weights(query, key_rows, same)
    weights = weights32.astype(jnp.bfloat16)
    attended = jnp.einsum(
        "phfg,gphd->fphd", weights, value_rows, preferred_element_type=jnp.float32
    ).astype(jnp.bfloat16)
    att_rows = attended.reshape(frames * local_patches, inner)
    out_grad = reduce_out(contract_rows(att_rows, cot_rows))
    mixed = jnp.dot(att_rows, out_weight, preferred_element_type=jnp.float32).astype(jnp.bfloat16)
    mixed = to_frames(mixed.reshape(1, frames, local_patches, width))
    grad_att = contract_cols(cot_rows, out_weight).astype(jnp.bfloat16)
    grad_heads = grad_att.reshape(frames, local_patches, HEADS, HD)
    grad_weights = jnp.einsum(
        "fphd,gphd->phfg", grad_heads, value_rows, preferred_element_type=jnp.float32
    )
    grad_values = jnp.einsum(
        "phfg,fphd->gphd", weights, grad_heads, preferred_element_type=jnp.float32
    ).astype(jnp.bfloat16)
    totals = jnp.sum(weights32 * grad_weights, axis=-1, keepdims=True)
    scale = 1.0 / jnp.sqrt(jnp.float32(HD))
    grad_scores = (weights32 * (grad_weights - totals) * scale).astype(jnp.bfloat16)
    grad_query = jnp.einsum(
        "phfg,gphd->fphd", grad_scores, key_rows, preferred_element_type=jnp.float32
    ).astype(jnp.bfloat16)
    grad_keys = jnp.einsum(
        "phfg,fphd->gphd", grad_scores, query, preferred_element_type=jnp.float32
    ).astype(jnp.bfloat16)
    grad_proj = jnp.stack([grad_query, grad_keys, grad_values], axis=2)
    grad_rows = grad_proj.reshape(frames * local_patches, 3 * inner)
    grad_latents = contract_cols(grad_rows, in_weight).astype(jnp.bfloat16)
    grad_latents = to_frames(grad_latents.reshape(1, frames, local_patches, width))
    return (mixed.reshape(latents.shape), grad_latents.reshape(latents.shape), out_grad)


ROWS = 64
PAIRS = 16
TILE = 128
INNER = HEADS * HD
PIECE = 41 * 8
SMEM = pl.BlockSpec(memory_space=pltpu.SMEM)
VMEM = pl.BlockSpec(memory_space=pltpu.VMEM)
HBM = pl.BlockSpec(memory_space=pltpu.HBM)
CHUNKS = ((0, 256), (256, 256), (512, 256), (768, 256), (1024, 128))


def shaped(shape, dtype=jnp.bfloat16):
    return jax.ShapeDtypeStruct(shape, dtype)


def dot(left, right):
    return jnp.dot(left, right, preferred_element_type=jnp.float32)


def flat(value):
    return value.reshape(value.shape[0] * ROWS, value.shape[2])


def call(kernel, scalars, inputs, outs, scratch=(), limit=8, flops=10**6, to_hbm=False, size=None, same=None):
    size = size or sum(x.size * x.dtype.itemsize for x in (*inputs, *outs))
    return pl.pallas_call(
        kernel,
        out_shape=list(outs),
        in_specs=[SMEM] * len(scalars) + [VMEM] * len(inputs),
        out_specs=[HBM if to_hbm else VMEM] * len(outs),
        scratch_shapes=[x if hasattr(x, "memory_space") else pltpu.VMEM(*x) for x in scratch],
        input_output_aliases={len(scalars) + same[0]: same[1]} if same else {},
        compiler_params=pltpu.CompilerParams(vmem_limit_bytes=limit << 20),
        cost_estimate=pl.CostEstimate(flops=flops, bytes_accessed=size, transcendentals=0),
    )(*scalars, *inputs)


def roles(spot):
    zpos, lens = spot[0] // 2, [spot[2 + i] for i in range(3)]
    first = 2 * zpos
    ends = [lens[0], lens[0] + lens[1], lens[0] + lens[1] + lens[2]]
    long = jnp.where(
        lens[0] == 4, 0, jnp.where(lens[1] == 4, ends[0], jnp.where(lens[2] == 4, ends[1], ends[2]))
    )

    def clip(frame):
        return sum((end <= frame).astype(jnp.int32) for end in ends)

    ids = [
        jnp.where(zpos == 0, -1, clip(first - 1)),
        clip(first),
        clip(first + 1),
        jnp.where(zpos == 3, -2, clip(first + 2)),
    ]
    return {
        "core": spot[0] % 2,
        "odd": zpos % 2,
        "left": 6 - 2 * (zpos % 2),
        "right": 4 + 2 * (zpos % 2),
        "ids": ids,
        "low": long == first,
        "high": long == first - 2,
        "middle": long == first - 1,
        "tail": long == first - 3,
        "head": long == first + 1,
    }


def slots(role, window):
    low, high, left, right = role["low"], role["high"], role["left"], role["right"]
    in_low = ((0, 2, right, right + 1), (1, 3, left, left + 1))[window]
    in_high = ((left, left + 1, 1, 3), (0, 2, right, right + 1))[window]
    usual = (left + window, window, 2 + window, right + window)
    blocks = [
        jnp.where(low, a, jnp.where(high, b, c)) for a, b, c in zip(in_low, in_high, usual)
    ]
    even, middle = low | high, role["middle"]
    odd = [middle, ~even & ~role["tail"], ~even & ~role["head"], middle]
    return blocks, [even | x for x in odd] if window == 0 else odd


def pick_kernel(spot, own, sib, near, far, both):
    role = roles(spot)
    core, odd = role["core"], role["odd"]
    for i in range(2):
        both[2 * core + i] = own[i if own.shape[0] == 2 else 2 * core + i]
        both[2 * (1 - core) + i] = sib[2 * core + i]
    right = (jnp.where(role["low"], 1, 2), 3)
    left = (0, jnp.where(role["high"], 2, 1))
    for i in range(2):
        near[i] = both[jnp.where(odd == 1, left[i], right[i])]
        far[i] = both[jnp.where(odd == 1, right[i], left[i])]


def early_kernel(lat_ab, wi_ref, qkv_ref):
    x = flat(lat_ab[...])
    for j in range(3):
        cols = slice(j * INNER, (j + 1) * INNER)
        qkv_ref[:4, :, cols] = dot(x, wi_ref[:, cols]).astype(jnp.bfloat16).reshape(4, ROWS, INNER)


def pair(f, g, w=0, count=1):
    start = (4 * f + g) * 2 * ROWS + w * ROWS
    return slice(start, start + count * ROWS)


def lanes(t, offset=0):
    return slice(offset + TILE * t, offset + TILE * (t + 1))


def forward_kernel(
    spot, far, near, wi_ref, _, heads_ref, qkv_ref, att_ref, p_ref, wide_ref,
    x_scr, hi_scr, w_scr,
):
    x_scr[:2] = near[...]
    x_scr[2:] = far[...]
    x = flat(x_scr[...])
    for j in range(3):
        cols = slice(j * INNER, (j + 1) * INNER)
        qkv_ref[4:, :, cols] = dot(x, wi_ref[:, cols]).astype(jnp.bfloat16).reshape(4, ROWS, INNER)
    role = roles(spot)
    even, ids = role["low"] | role["high"], role["ids"]
    windows = [slots(role, w) for w in range(2)]
    for w, (blocks, _) in enumerate(windows):
        for t in range(INNER // TILE):
            q = [qkv_ref[blocks[f], :, lanes(t)] for f in range(4)]
            k = [qkv_ref[blocks[g], :, lanes(t, INNER)] for g in range(4)]
            for f in range(4):
                for g in range(4):
                    hi_scr[pair(f, g, w), lanes(t)] = q[f] * k[g]
    scores = contract_cols(heads_ref[...], hi_scr[...])
    for f in range(4):
        line = []
        for g in range(4):
            bias = jnp.where(even | (ids[f] == ids[g]), 0.0, -jnp.inf)
            line.append(scores[:, pair(f, g, 0, 2)] * HD**-0.5 + bias)
        top = jnp.maximum(jnp.maximum(line[0], line[1]), jnp.maximum(line[2], line[3]))
        line = [jnp.exp(x - top) for x in line]
        share = 1.0 / (line[0] + line[1] + line[2] + line[3])
        for g in range(4):
            p_ref[:, pair(f, g, 0, 2)] = line[g] * share
    w_scr[...] = p_ref[...].T.astype(jnp.bfloat16)
    for f in range(4):
        rows = pair(f, 0, 0, 8)
        for start, size in CHUNKS:
            cols = slice(start, start + size)
            spread = dot(w_scr[rows, :], heads_ref[:, cols])
            wide_ref[rows, cols] = spread.astype(jnp.bfloat16)
            for w, (blocks, kept) in enumerate(windows):
                base = 2 * INNER + start
                total = sum(
                    spread[pair(0, g, w)] * qkv_ref[blocks[g], :, base : base + size].astype(jnp.float32)
                    for g in range(4)
                )
                total = total * jnp.where(kept[f], 1.0, 0.0)
                att_ref[blocks[f], :, cols] = total.astype(jnp.bfloat16)


def part_rows(core, att_t, cot, rows):
    height = att_t.shape[0] // 8
    for z in range(4):
        start = pl.multiple_of((2 * z + core) * height, 16)
        rows[z * height : (z + 1) * height, :] = att_t[pl.ds(start, height), :]
    return dot(rows[...], flat(cot[...])).reshape(4, height, -1)


def part_kernel(spot, att_ref, ab_ref, far, near, sib_ref, att_t, cot, rows):
    cot[:4] = ab_ref[...]
    cot[4:6] = near[...]
    cot[6:] = far[...]
    att_t[...] = flat(att_ref[...]).T
    sib_ref[...] = part_rows(1 - spot[0] % 2, att_t, cot, rows).astype(jnp.bfloat16)


def mix_kernel(att_ref, w_ref, here_ref, near_ref, far_ref):
    made = dot(flat(att_ref[...]), w_ref[...]).astype(jnp.bfloat16).reshape(8, ROWS, -1)
    here_ref[...] = made[:4]
    near_ref[...] = made[4:6]
    far_ref[...] = made[6:]


def grad_att_kernel(cot, wo_ref, *refs, first):
    rows = cot[first : first + 4]
    made = contract_cols(flat(rows), wo_ref[...])
    refs[-1][first : first + 4] = made.astype(jnp.bfloat16).reshape(4, ROWS, INNER)


def backward_kernel(
    spot, ga_ref, qkv_ref, p_ref, wide_ref, heads_ref, d_ref, hi_scr, t_scr, s_scr
):
    role = roles(spot)
    windows = [slots(role, w)[0] for w in range(2)]
    for w, blocks in enumerate(windows):
        for t in range(INNER // TILE):
            do = [ga_ref[blocks[f], :, lanes(t)] for f in range(4)]
            v = [qkv_ref[blocks[g], :, lanes(t, 2 * INNER)] for g in range(4)]
            for f in range(4):
                for g in range(4):
                    hi_scr[pair(f, g, w), lanes(t)] = do[f] * v[g]
    grads = contract_cols(heads_ref[...], hi_scr[...])
    for f in range(4):
        p = [p_ref[:, pair(f, g, 0, 2)] for g in range(4)]
        line = [grads[:, pair(f, g, 0, 2)] for g in range(4)]
        total = sum(p[g] * line[g] for g in range(4))
        for g in range(4):
            t_scr[:, pair(f, g, 0, 2)] = p[g] * (line[g] - total) * HD**-0.5
    s_scr[...] = t_scr[...].T.astype(jnp.bfloat16)
    for start, size in CHUNKS:
        cols = slice(start, start + size)
        spread = dot(s_scr[...], heads_ref[:, cols])
        for w, blocks in enumerate(windows):

            def take(ref, block, offset=0):
                return ref[block, :, offset + start : offset + start + size].astype(jnp.float32)

            def put(block, offset, value):
                d_ref[block, :, offset + start : offset + start + size] = value.astype(jnp.bfloat16)

            do = [take(ga_ref, blocks[f]) for f in range(4)]
            for g in range(4):
                put(
                    blocks[g], 2 * INNER,
                    sum(wide_ref[pair(f, g, w), cols].astype(jnp.float32) * do[f] for f in range(4)),
                )
            q = [take(qkv_ref, blocks[f]) for f in range(4)]
            k = [take(qkv_ref, blocks[g], INNER) for g in range(4)]
            for f in range(4):
                put(blocks[f], 0, sum(spread[pair(f, g, w)] * k[g] for g in range(4)))
            for g in range(4):
                put(blocks[g], INNER, sum(spread[pair(f, g, w)] * q[f] for f in range(4)))


def latents_kernel(d_ref, wi_ref, *outs, first):
    tile = 384
    for j in range(wi_ref.shape[0] // tile):
        cols = slice(j * tile, (j + 1) * tile)
        made = contract_cols(flat(d_ref[first : first + 4]), wi_ref[cols, :]).astype(jnp.bfloat16)
        made = made.reshape(4, ROWS, tile)
        size = 4 // len(outs)
        for i, out in enumerate(outs):
            out[:, :, cols] = made[i * size : (i + 1) * size]


def settle_kernel(spot, *refs):
    *given, own, sib = refs
    role = roles(spot)
    core, left, right = role["core"], role["left"], role["right"]
    low, high, tail, head = role["low"], role["high"], role["tail"], role["head"]
    where = [
        jnp.where(high | tail, left, 0),
        jnp.where(low, right, jnp.where(tail, left + 1, 1)),
        jnp.where(high, left + 1, jnp.where(head, right, 2)),
        jnp.where(low | head, right + 1, 3),
    ]

    def put(out, row, block, here, far, near):
        for source, first, count in ((here, 0, 4), (near, 4, 2), (far, 6, 2)):

            @pl.when((block >= first) & (block < first + count))
            def _():
                out[row] = source[block - first]

    for base in (0, 2):
        sources = given[:3] if base == 0 else given[3:]
        for i in range(2):
            put(own, base + i, jnp.where(core == 0, where[i], where[2 + i]), *sources)
            put(sib, base + i, jnp.where(core == 0, where[2 + i], where[i]), *sources)


def first_row(group, block):
    return pl.multiple_of((group * 81 // 2 + block * 162) * 8, 8)


def mine_kernel(spot, att_t, cot, total, rows):
    height, width = att_t.shape[0] // 8, cot.shape[2]
    made = part_rows(spot[0] % 2, att_t, cot, rows)
    for z in range(4):
        for t in range(width // TILE):
            start = (z * width // TILE + t) * height
            total[start : start + height, :] = made[z][:, lanes(t)]


def cores_kernel(spot, mine, got, keep, *sends):
    group = spot[1]
    *sends, total = sends
    height, width = got.shape[1:]
    for z in range(4):
        for t in range(width // TILE):
            rows = slice((z * width // TILE + t) * height, (z * width // TILE + t + 1) * height)
            total[rows, :] = mine[rows, :] + got[z, :, lanes(t)].astype(jnp.float32)
    for flip, out in enumerate((keep, *sends)):
        for z in range(4):
            out[z] = total[pl.ds(first_row(group ^ flip, z), PIECE), :].astype(out.dtype)


def groups_kernel(spot, own, one, two, three, keep, *sends):
    zpos = spot[0] // 2
    *sends, total = sends
    total[...] = own[...] + sum(x[...].astype(jnp.float32) for x in (one, two, three))
    for flip, out in enumerate((keep, *sends)):
        out[...] = total[zpos ^ flip].astype(out.dtype)


def chips_kernel(own, one, two, three, out):
    total = own[...] + sum(x[...].astype(jnp.float32) for x in (one, two, three))
    out[...] = total.astype(jnp.bfloat16)


def gather_kernel(spot, own, one, two, three, out, held, rows):
    for flip, value in enumerate((own, one, two, three)):
        held[spot[1] ^ flip] = value[...].astype(jnp.float32)
    for group in range(4):
        rows[pl.ds(first_row(group, 0), PIECE), :] = held[group]
    height, width = out.shape
    for t in range(width // TILE):
        out[:, lanes(t)] = rows[t * height : (t + 1) * height, :]


def final_kernel(spot, own, sib, rows, mixed, grad, out, sems):
    core = spot[0] % 2
    here, there = pl.ds(2 * core, 2), pl.ds(2 * (1 - core), 2)
    moves = [(rows.at[i : i + 48], out.at[i : i + 48]) for i in range(0, out.shape[0], 48)]
    for base, made in ((0, mixed), (2, grad)):
        moves.append((own.at[base : base + 2], made.at[here]))
        moves.append((sib.at[base : base + 2], made.at[there]))
    copies = [pltpu.make_async_copy(x, y, sems.at[i]) for i, (x, y) in enumerate(moves)]
    for copy in copies:
        copy.start()
    for copy in copies:
        copy.wait()


def after(later, earlier):
    return lax.optimization_barrier((later, earlier))


def exchange(near, far):
    pairs = [(0, 0), (1, 1), (2, 4), (4, 2), (3, 5), (5, 3), (6, 6), (7, 7)]
    return lax.ppermute(far, "seq", pairs), swap(near, "seq", 2)


def clip_body(latents, in_weight, out_weight, cotangent, clip_lengths):
    width = latents.shape[3]
    rows = INNER // 8
    wide = jnp.float32
    place = jnp.arange(2 + clip_lengths.shape[1], dtype=jnp.int32)
    spot = jnp.where(place == 0, lax.axis_index("seq"), jnp.where(place == 1, lax.axis_index("dp"), 0))
    spot = spot + jnp.pad(clip_lengths[0], (2, 0))
    heads = jnp.asarray(np.arange(INNER) // HD == np.arange(HEADS)[:, None], jnp.bfloat16)
    lat = latents.reshape(4, ROWS, width)
    cot = cotangent.reshape(4, ROWS, width)

    bf16 = jnp.bfloat16
    four, two, eight = shaped((4, ROWS, width)), shaped((2, ROWS, width)), shaped((8, ROWS, INNER))

    def pick(own, sib, flops):
        near, far, both = call(pick_kernel, [spot], [own, sib], [two, two, four], flops=flops)
        return exchange(near, far), both

    lat_sib, cot_sib = swap(lat, "seq", 1), swap(cot, "seq", 1)
    lat_own = lax.dynamic_slice_in_dim(lat, 2 * (lax.axis_index("seq") % 2), 2, 0)
    (lat_far, lat_near), lat_ab = pick(lat_own, lat_sib, 4 * 10**9)
    (qkv_ab,) = call(
        early_kernel, [], [lat_ab, in_weight], [shaped((8, ROWS, 3 * INNER))], limit=16, flops=27 * 10**8
    )
    cot_sib, qkv_ab = after(cot_sib, qkv_ab)
    (cot_far, cot_near), cot_ab = pick(cot, cot_sib, 10**6)
    grad_att = functools.partial(grad_att_kernel, first=0)
    (ga,) = call(grad_att, [], [cot_ab, out_weight], [eight], limit=16, flops=7 * 10**8)
    lat_far, ga = after(lat_far, ga)
    pairs = 2 * PAIRS * ROWS
    products, columns = ((pairs, INNER), bf16), ((pairs, HEADS), bf16)
    qkv, att, probs, wides = call(
        forward_kernel, [spot], [lat_far, lat_near, in_weight, qkv_ab, heads],
        [shaped((8, ROWS, 3 * INNER)), eight, shaped((HEADS, pairs), wide), shaped((pairs, INNER))],
        [((4, ROWS, width), bf16), products, columns], limit=24, flops=8 * 10**9, same=(3, 0),
    )
    part_scr = ((4 * rows, 8 * ROWS), bf16)
    other, att_t, cot_all = call(
        part_kernel, [spot], [att, cot_ab, cot_far, cot_near],
        [shaped((4, rows, width)), shaped((INNER, 8 * ROWS)), eight], [part_scr],
        limit=16, flops=7 * 10**8,
    )
    got = swap(other, "seq", 1)
    cot_all, other = after(cot_all, other)
    grad_att = functools.partial(grad_att_kernel, first=4)
    (ga,) = call(grad_att, [], [cot_all, out_weight, ga], [eight], limit=16, flops=7 * 10**8, same=(2, 0))
    part, piece = (4, PIECE, TILE), (PIECE, TILE)
    tiles = rows * width // TILE
    (mine,) = call(
        mine_kernel, [spot], [att_t, cot_all], [shaped((4 * tiles, TILE), wide)], [part_scr],
        limit=16, flops=7 * 10**8,
    )
    mine, ga = after(mine, ga)
    keep, *sends = call(
        cores_kernel, [spot], [mine, got], [shaped(part, wide)] + [shaped(part)] * 3,
        [((4 * tiles, TILE), wide)], limit=16, flops=7 * 10**8,
    )
    att, sends = after(att, sends)
    sends = [swap(sends[flip - 1], "dp", flip) for flip in (3, 1, 2)]
    mixed = call(mix_kernel, [], [att, out_weight], [four, two, two], limit=16, size=10**3)
    qkv, mixed = after(qkv, mixed)
    mixed = [mixed[0], *exchange(mixed[1], mixed[2])]
    (d_all,) = call(
        backward_kernel, [spot], [ga, qkv, probs, wides, heads], [shaped((8, ROWS, 3 * INNER))],
        [products, ((HEADS, pairs), wide), columns], limit=24, size=10**3,
    )
    theirs = functools.partial(latents_kernel, first=4)
    grad = call(theirs, [], [d_all, in_weight], [two, two], limit=16, size=10**3)
    keep, (grad, mixed) = after(keep, (grad, mixed))
    keep, *sends = call(
        groups_kernel, [spot], [keep, *sends], [shaped(piece, wide)] + [shaped(piece)] * 3,
        [(part, wide)],
    )
    grad, keep = after(grad, keep)
    sends = [swap(x, "seq", 2 * flip) for flip, x in enumerate(sends, 1)]
    d_all, grad = after(d_all, grad)
    ours = functools.partial(latents_kernel, first=0)
    (own,) = call(ours, [], [d_all, in_weight], [four], limit=16, flops=8 * 10**9)
    grad = [own, *exchange(grad[0], grad[1])]
    keep, grad[0] = after(keep, grad[0])
    (last,) = call(chips_kernel, [], [keep, *sends], [shaped(piece)])
    grad[0], last = after(grad[0], last)
    others = [swap(last, "dp", flip) for flip in (1, 2, 3)]
    own, sib = call(settle_kernel, [spot], [*mixed, *grad], [four, four])
    (out_grad,) = call(
        gather_kernel, [spot], [last, *others], [shaped((rows, width), wide)],
        [(part, wide), ((tiles, TILE), wide)], flops=8 * 10**9,
    )
    mixed, grad, out_grad = call(
        final_kernel, [spot], [own, swap(sib, "seq", 1), out_grad],
        [four, four, shaped((rows, width), wide)], [pltpu.SemaphoreType.DMA((7,))], to_hbm=True,
    )
    return mixed.reshape(latents.shape), grad.reshape(latents.shape), out_grad


def body(latents, *others):
    frames, patches = latents.shape[1] * lax.axis_size("seq"), latents.shape[2]
    small = (lax.axis_size("dp"), lax.axis_size("seq"), frames, patches) == (4, 8, 8, 4 * ROWS)
    return (clip_body if small else patch_body)(latents, *others)


def solution(mesh):
    placed = (P("dp", "seq", None, None), P(), P(), P("dp", "seq", None, None), P("dp", None))
    return jax.shard_map(
        body,
        mesh=mesh,
        in_specs=placed,
        out_specs=(P("dp", "seq", None, None), P("dp", "seq", None, None), P("seq", None)),
        check_vma=False,
    )
```

```python
import functools

import jax
import jax.numpy as jnp
import numpy as np
from jax import lax
from jax.experimental import pallas as pl
from jax.experimental.pallas import tpu as pltpu
from jax.sharding import PartitionSpec as P

HEADS = 16
HD = 72


def clip_index(lengths, frames):
    ends = jnp.cumsum(lengths)
    position = jnp.arange(frames, dtype=jnp.int32)
    return jnp.sum((ends[None, :] <= position[:, None]).astype(jnp.int32), axis=1)


def softmax_weights(query, key_rows, same):
    scale = 1.0 / jnp.sqrt(jnp.float32(HD))
    scores = (
        jnp.einsum("fphd,gphd->phfg", query, key_rows, preferred_element_type=jnp.float32) * scale
    )
    scores = jnp.where(same[None, None], scores, -jnp.inf)
    return jax.nn.softmax(scores, axis=-1)


def contract_rows(left, right):
    return lax.dot_general(
        left, right, (((0,), (0,)), ((), ())), preferred_element_type=jnp.float32
    )


def contract_cols(left, right):
    return lax.dot_general(
        left, right, (((1,), (1,)), ((), ())), preferred_element_type=jnp.float32
    )


def swap(value, axis, flip):
    size = lax.axis_size(axis)
    return lax.ppermute(value, axis, [(i, i ^ flip) for i in range(size)])


def reduce_out(part):
    mine = lax.psum_scatter(part, "seq", scatter_dimension=0, tiled=True)
    return lax.psum(mine.astype(jnp.bfloat16), "dp").astype(jnp.float32)


def patch_body(latents, in_weight, out_weight, cotangent, clip_lengths):
    shards = lax.axis_size("seq")
    local_frames = latents.shape[1]
    patches = latents.shape[2]
    width = latents.shape[3]
    frames = local_frames * shards
    local_patches = patches // shards
    inner = HEADS * HD

    def to_patches(rows):
        return lax.all_to_all(rows, "seq", split_axis=2, concat_axis=1, tiled=True)

    def to_frames(rows):
        return lax.all_to_all(rows, "seq", split_axis=1, concat_axis=2, tiled=True)

    lat_rows = to_patches(latents).reshape(frames * local_patches, width)
    cot_rows = to_patches(cotangent).reshape(frames * local_patches, width)
    projected = jnp.dot(lat_rows, in_weight, preferred_element_type=jnp.float32).astype(
        jnp.bfloat16
    )
    split = projected.reshape(frames, local_patches, 3, HEADS, HD)
    query, key_rows, value_rows = (split[:, :, 0], split[:, :, 1], split[:, :, 2])
    clip = clip_index(clip_lengths[0], frames)
    same = clip[:, None] == clip[None, :]
    weights32 = softmax_weights(query, key_rows, same)
    weights = weights32.astype(jnp.bfloat16)
    attended = jnp.einsum(
        "phfg,gphd->fphd", weights, value_rows, preferred_element_type=jnp.float32
    ).astype(jnp.bfloat16)
    att_rows = attended.reshape(frames * local_patches, inner)
    out_grad = reduce_out(contract_rows(att_rows, cot_rows))
    mixed = jnp.dot(att_rows, out_weight, preferred_element_type=jnp.float32).astype(jnp.bfloat16)
    mixed = to_frames(mixed.reshape(1, frames, local_patches, width))
    grad_att = contract_cols(cot_rows, out_weight).astype(jnp.bfloat16)
    grad_heads = grad_att.reshape(frames, local_patches, HEADS, HD)
    grad_weights = jnp.einsum(
        "fphd,gphd->phfg", grad_heads, value_rows, preferred_element_type=jnp.float32
    )
    grad_values = jnp.einsum(
        "phfg,fphd->gphd", weights, grad_heads, preferred_element_type=jnp.float32
    ).astype(jnp.bfloat16)
    totals = jnp.sum(weights32 * grad_weights, axis=-1, keepdims=True)
    scale = 1.0 / jnp.sqrt(jnp.float32(HD))
    grad_scores = (weights32 * (grad_weights - totals) * scale).astype(jnp.bfloat16)
    grad_query = jnp.einsum(
        "phfg,gphd->fphd", grad_scores, key_rows, preferred_element_type=jnp.float32
    ).astype(jnp.bfloat16)
    grad_keys = jnp.einsum(
        "phfg,fphd->gphd", grad_scores, query, preferred_element_type=jnp.float32
    ).astype(jnp.bfloat16)
    grad_proj = jnp.stack([grad_query, grad_keys, grad_values], axis=2)
    grad_rows = grad_proj.reshape(frames * local_patches, 3 * inner)
    grad_latents = contract_cols(grad_rows, in_weight).astype(jnp.bfloat16)
    grad_latents = to_frames(grad_latents.reshape(1, frames, local_patches, width))
    return (mixed.reshape(latents.shape), grad_latents.reshape(latents.shape), out_grad)


ROWS = 64
PAIRS = 16
TILE = 128
INNER = HEADS * HD
PIECE = 41 * 8
SMEM = pl.BlockSpec(memory_space=pltpu.SMEM)
VMEM = pl.BlockSpec(memory_space=pltpu.VMEM)
HBM = pl.BlockSpec(memory_space=pltpu.HBM)
CHUNKS = ((0, 256), (256, 256), (512, 256), (768, 256), (1024, 128))


def shaped(shape, dtype=jnp.bfloat16):
    return jax.ShapeDtypeStruct(shape, dtype)


def dot(left, right):
    return jnp.dot(left, right, preferred_element_type=jnp.float32)


def flat(value):
    return value.reshape(value.shape[0] * ROWS, value.shape[2])


def call(kernel, scalars, inputs, outs, scratch=(), limit=8, flops=10**6, to_hbm=False, size=None, same=None):
    size = size or sum(x.size * x.dtype.itemsize for x in (*inputs, *outs))
    return pl.pallas_call(
        kernel,
        out_shape=list(outs),
        in_specs=[SMEM] * len(scalars) + [VMEM] * len(inputs),
        out_specs=[HBM if to_hbm else VMEM] * len(outs),
        scratch_shapes=[x if hasattr(x, "memory_space") else pltpu.VMEM(*x) for x in scratch],
        input_output_aliases={len(scalars) + same[0]: same[1]} if same else {},
        compiler_params=pltpu.CompilerParams(vmem_limit_bytes=limit << 20),
        cost_estimate=pl.CostEstimate(flops=flops, bytes_accessed=size, transcendentals=0),
    )(*scalars, *inputs)


def roles(spot):
    zpos, lens = spot[0] // 2, [spot[2 + i] for i in range(3)]
    first = 2 * zpos
    ends = [lens[0], lens[0] + lens[1], lens[0] + lens[1] + lens[2]]
    long = jnp.where(
        lens[0] == 4, 0, jnp.where(lens[1] == 4, ends[0], jnp.where(lens[2] == 4, ends[1], ends[2]))
    )

    def clip(frame):
        return sum((end <= frame).astype(jnp.int32) for end in ends)

    ids = [
        jnp.where(zpos == 0, -1, clip(first - 1)),
        clip(first),
        clip(first + 1),
        jnp.where(zpos == 3, -2, clip(first + 2)),
    ]
    return {
        "core": spot[0] % 2,
        "odd": zpos % 2,
        "left": 6 - 2 * (zpos % 2),
        "right": 4 + 2 * (zpos % 2),
        "ids": ids,
        "low": long == first,
        "high": long == first - 2,
        "middle": long == first - 1,
        "tail": long == first - 3,
        "head": long == first + 1,
    }


def slots(role, window):
    low, high, left, right = role["low"], role["high"], role["left"], role["right"]
    in_low = ((0, 2, right, right + 1), (1, 3, left, left + 1))[window]
    in_high = ((left, left + 1, 1, 3), (0, 2, right, right + 1))[window]
    usual = (left + window, window, 2 + window, right + window)
    blocks = [
        jnp.where(low, a, jnp.where(high, b, c)) for a, b, c in zip(in_low, in_high, usual)
    ]
    even, middle = low | high, role["middle"]
    odd = [middle, ~even & ~role["tail"], ~even & ~role["head"], middle]
    return blocks, [even | x for x in odd] if window == 0 else odd


def pick_kernel(spot, own, sib, near, far, both):
    role = roles(spot)
    core, odd = role["core"], role["odd"]
    for i in range(2):
        both[2 * core + i] = own[i if own.shape[0] == 2 else 2 * core + i]
        both[2 * (1 - core) + i] = sib[2 * core + i]
    right = (jnp.where(role["low"], 1, 2), 3)
    left = (0, jnp.where(role["high"], 2, 1))
    for i in range(2):
        near[i] = both[jnp.where(odd == 1, left[i], right[i])]
        far[i] = both[jnp.where(odd == 1, right[i], left[i])]


def early_kernel(lat_ab, wi_ref, qkv_ref):
    x = flat(lat_ab[...])
    for j in range(3):
        cols = slice(j * INNER, (j + 1) * INNER)
        qkv_ref[:4, :, cols] = dot(x, wi_ref[:, cols]).astype(jnp.bfloat16).reshape(4, ROWS, INNER)


def pair(f, g, w=0, count=1):
    start = (4 * f + g) * 2 * ROWS + w * ROWS
    return slice(start, start + count * ROWS)


def lanes(t, offset=0):
    return slice(offset + TILE * t, offset + TILE * (t + 1))


def forward_kernel(
    spot, far, near, wi_ref, _, heads_ref, qkv_ref, att_ref, p_ref, wide_ref,
    x_scr, hi_scr, w_scr,
):
    x_scr[:2] = near[...]
    x_scr[2:] = far[...]
    x = flat(x_scr[...])
    for j in range(3):
        cols = slice(j * INNER, (j + 1) * INNER)
        qkv_ref[4:, :, cols] = dot(x, wi_ref[:, cols]).astype(jnp.bfloat16).reshape(4, ROWS, INNER)
    role = roles(spot)
    even, ids = role["low"] | role["high"], role["ids"]
    windows = [slots(role, w) for w in range(2)]
    for w, (blocks, _) in enumerate(windows):
        for t in range(INNER // TILE):
            q = [qkv_ref[blocks[f], :, lanes(t)] for f in range(4)]
            k = [qkv_ref[blocks[g], :, lanes(t, INNER)] for g in range(4)]
            for f in range(4):
                for g in range(4):
                    hi_scr[pair(f, g, w), lanes(t)] = q[f] * k[g]
    scores = contract_cols(heads_ref[...], hi_scr[...])
    for f in range(4):
        line = []
        for g in range(4):
            bias = jnp.where(even | (ids[f] == ids[g]), 0.0, -jnp.inf)
            line.append(scores[:, pair(f, g, 0, 2)] * HD**-0.5 + bias)
        top = jnp.maximum(jnp.maximum(line[0], line[1]), jnp.maximum(line[2], line[3]))
        line = [jnp.exp(x - top) for x in line]
        share = 1.0 / (line[0] + line[1] + line[2] + line[3])
        for g in range(4):
            p_ref[:, pair(f, g, 0, 2)] = line[g] * share
    w_scr[...] = p_ref[...].T.astype(jnp.bfloat16)
    for f in range(4):
        rows = pair(f, 0, 0, 8)
        for start, size in CHUNKS:
            cols = slice(start, start + size)
            spread = dot(w_scr[rows, :], heads_ref[:, cols])
            wide_ref[rows, cols] = spread.astype(jnp.bfloat16)
            for w, (blocks, kept) in enumerate(windows):
                base = 2 * INNER + start
                total = sum(
                    spread[pair(0, g, w)] * qkv_ref[blocks[g], :, base : base + size].astype(jnp.float32)
                    for g in range(4)
                )
                total = total * jnp.where(kept[f], 1.0, 0.0)
                att_ref[blocks[f], :, cols] = total.astype(jnp.bfloat16)


def part_rows(core, att_t, cot, rows):
    height = att_t.shape[0] // 8
    for z in range(4):
        start = pl.multiple_of((2 * z + core) * height, 16)
        rows[z * height : (z + 1) * height, :] = att_t[pl.ds(start, height), :]
    return dot(rows[...], flat(cot[...])).reshape(4, height, -1)


def part_kernel(spot, att_ref, ab_ref, far, near, sib_ref, att_t, cot, rows):
    cot[:4] = ab_ref[...]
    cot[4:6] = near[...]
    cot[6:] = far[...]
    att_t[...] = flat(att_ref[...]).T
    sib_ref[...] = part_rows(1 - spot[0] % 2, att_t, cot, rows).astype(jnp.bfloat16)


def mix_kernel(att_ref, w_ref, here_ref, near_ref, far_ref):
    made = dot(flat(att_ref[...]), w_ref[...]).astype(jnp.bfloat16).reshape(8, ROWS, -1)
    here_ref[...] = made[:4]
    near_ref[...] = made[4:6]
    far_ref[...] = made[6:]


def grad_att_kernel(cot, wo_ref, *refs, first):
    rows = cot[first : first + 4]
    made = contract_cols(flat(rows), wo_ref[...])
    refs[-1][first : first + 4] = made.astype(jnp.bfloat16).reshape(4, ROWS, INNER)


def backward_kernel(
    spot, ga_ref, qkv_ref, p_ref, wide_ref, heads_ref, d_ref, hi_scr, t_scr, s_scr
):
    role = roles(spot)
    windows = [slots(role, w)[0] for w in range(2)]
    for w, blocks in enumerate(windows):
        for t in range(INNER // TILE):
            do = [ga_ref[blocks[f], :, lanes(t)] for f in range(4)]
            v = [qkv_ref[blocks[g], :, lanes(t, 2 * INNER)] for g in range(4)]
            for f in range(4):
                for g in range(4):
                    hi_scr[pair(f, g, w), lanes(t)] = do[f] * v[g]
    grads = contract_cols(heads_ref[...], hi_scr[...])
    for f in range(4):
        p = [p_ref[:, pair(f, g, 0, 2)] for g in range(4)]
        line = [grads[:, pair(f, g, 0, 2)] for g in range(4)]
        total = sum(p[g] * line[g] for g in range(4))
        for g in range(4):
            t_scr[:, pair(f, g, 0, 2)] = p[g] * (line[g] - total) * HD**-0.5
    s_scr[...] = t_scr[...].T.astype(jnp.bfloat16)
    for start, size in CHUNKS:
        cols = slice(start, start + size)
        spread = dot(s_scr[...], heads_ref[:, cols])
        for w, blocks in enumerate(windows):

            def take(ref, block, offset=0):
                return ref[block, :, offset + start : offset + start + size].astype(jnp.float32)

            def put(block, offset, value):
                d_ref[block, :, offset + start : offset + start + size] = value.astype(jnp.bfloat16)

            do = [take(ga_ref, blocks[f]) for f in range(4)]
            for g in range(4):
                put(
                    blocks[g], 2 * INNER,
                    sum(wide_ref[pair(f, g, w), cols].astype(jnp.float32) * do[f] for f in range(4)),
                )
            q = [take(qkv_ref, blocks[f]) for f in range(4)]
            k = [take(qkv_ref, blocks[g], INNER) for g in range(4)]
            for f in range(4):
                put(blocks[f], 0, sum(spread[pair(f, g, w)] * k[g] for g in range(4)))
            for g in range(4):
                put(blocks[g], INNER, sum(spread[pair(f, g, w)] * q[f] for f in range(4)))


def latents_kernel(d_ref, wi_ref, *outs, first):
    tile = 384
    for j in range(wi_ref.shape[0] // tile):
        cols = slice(j * tile, (j + 1) * tile)
        made = contract_cols(flat(d_ref[first : first + 4]), wi_ref[cols, :]).astype(jnp.bfloat16)
        made = made.reshape(4, ROWS, tile)
        size = 4 // len(outs)
        for i, out in enumerate(outs):
            out[:, :, cols] = made[i * size : (i + 1) * size]


def settle_kernel(spot, *refs):
    *given, own, sib = refs
    role = roles(spot)
    core, left, right = role["core"], role["left"], role["right"]
    low, high, tail, head = role["low"], role["high"], role["tail"], role["head"]
    where = [
        jnp.where(high | tail, left, 0),
        jnp.where(low, right, jnp.where(tail, left + 1, 1)),
        jnp.where(high, left + 1, jnp.where(head, right, 2)),
        jnp.where(low | head, right + 1, 3),
    ]

    def put(out, row, block, here, far, near):
        for source, first, count in ((here, 0, 4), (near, 4, 2), (far, 6, 2)):

            @pl.when((block >= first) & (block < first + count))
            def _():
                out[row] = source[block - first]

    for base in (0, 2):
        sources = given[:3] if base == 0 else given[3:]
        for i in range(2):
            put(own, base + i, jnp.where(core == 0, where[i], where[2 + i]), *sources)
            put(sib, base + i, jnp.where(core == 0, where[2 + i], where[i]), *sources)


def first_row(group, block):
    return pl.multiple_of((group * 81 // 2 + block * 162) * 8, 8)


def mine_kernel(spot, att_t, cot, total, rows):
    height, width = att_t.shape[0] // 8, cot.shape[2]
    made = part_rows(spot[0] % 2, att_t, cot, rows)
    for z in range(4):
        for t in range(width // TILE):
            start = (z * width // TILE + t) * height
            total[start : start + height, :] = made[z][:, lanes(t)]


def cores_kernel(spot, mine, got, keep, *sends):
    group = spot[1]
    *sends, total = sends
    height, width = got.shape[1:]
    for z in range(4):
        for t in range(width // TILE):
            rows = slice((z * width // TILE + t) * height, (z * width // TILE + t + 1) * height)
            total[rows, :] = mine[rows, :] + got[z, :, lanes(t)].astype(jnp.float32)
    for flip, out in enumerate((keep, *sends)):
        for z in range(4):
            out[z] = total[pl.ds(first_row(group ^ flip, z), PIECE), :].astype(out.dtype)


def groups_kernel(spot, own, one, two, three, keep, *sends):
    zpos = spot[0] // 2
    *sends, total = sends
    total[...] = own[...] + sum(x[...].astype(jnp.float32) for x in (one, two, three))
    for flip, out in enumerate((keep, *sends)):
        out[...] = total[zpos ^ flip].astype(out.dtype)


def chips_kernel(own, one, two, three, out):
    total = own[...] + sum(x[...].astype(jnp.float32) for x in (one, two, three))
    out[...] = total.astype(jnp.bfloat16)


def arrived_kernel(one, two, three, token):
    token[...] = (one[:16, :] + two[:16, :]) + three[:16, :]


def final_kernel(
    spot, own, sib, last, one, two, three, _, mixed, grad, out, held, rows, made, sems
):
    core = spot[0] % 2
    here, there = pl.ds(2 * core, 2), pl.ds(2 * (1 - core), 2)
    moves = []
    for base, result in ((0, mixed), (2, grad)):
        moves.append((own.at[base : base + 2], result.at[here]))
        moves.append((sib.at[base : base + 2], result.at[there]))
    copies = [pltpu.make_async_copy(x, y, sems.at[i]) for i, (x, y) in enumerate(moves)]
    for copy in copies:
        copy.start()
    for flip, value in enumerate((last, one, two, three)):
        held[spot[1] ^ flip] = value[...].astype(jnp.float32)
    for group in range(4):
        rows[pl.ds(first_row(group, 0), PIECE), :] = held[group]
    height, width = out.shape
    for t in range(width // TILE):
        made[:, lanes(t)] = rows[t * height : (t + 1) * height, :]
    copies.append(pltpu.make_async_copy(made, out, sems.at[len(copies)]))
    copies[-1].start()
    for copy in copies:
        copy.wait()


def after(later, earlier):
    return lax.optimization_barrier((later, earlier))


def exchange(near, far):
    pairs = [(0, 0), (1, 1), (2, 4), (4, 2), (3, 5), (5, 3), (6, 6), (7, 7)]
    return lax.ppermute(far, "seq", pairs), swap(near, "seq", 2)


def clip_body(latents, in_weight, out_weight, cotangent, clip_lengths):
    width = latents.shape[3]
    rows = INNER // 8
    wide = jnp.float32
    place = jnp.arange(2 + clip_lengths.shape[1], dtype=jnp.int32)
    spot = jnp.where(place == 0, lax.axis_index("seq"), jnp.where(place == 1, lax.axis_index("dp"), 0))
    spot = spot + jnp.pad(clip_lengths[0], (2, 0))
    heads = jnp.asarray(np.arange(INNER) // HD == np.arange(HEADS)[:, None], jnp.bfloat16)
    lat = latents.reshape(4, ROWS, width)
    cot = cotangent.reshape(4, ROWS, width)

    bf16 = jnp.bfloat16
    four, two, eight = shaped((4, ROWS, width)), shaped((2, ROWS, width)), shaped((8, ROWS, INNER))

    def pick(own, sib, flops):
        near, far, both = call(pick_kernel, [spot], [own, sib], [two, two, four], flops=flops)
        return exchange(near, far), both

    lat_sib, cot_sib = swap(lat, "seq", 1), swap(cot, "seq", 1)
    lat_own = lax.dynamic_slice_in_dim(lat, 2 * (lax.axis_index("seq") % 2), 2, 0)
    (lat_far, lat_near), lat_ab = pick(lat_own, lat_sib, 4 * 10**9)
    (qkv_ab,) = call(
        early_kernel, [], [lat_ab, in_weight], [shaped((8, ROWS, 3 * INNER))], limit=16, flops=27 * 10**8
    )
    cot_sib, qkv_ab = after(cot_sib, qkv_ab)
    (cot_far, cot_near), cot_ab = pick(cot, cot_sib, 10**6)
    grad_att = functools.partial(grad_att_kernel, first=0)
    (ga,) = call(grad_att, [], [cot_ab, out_weight], [eight], limit=16, flops=7 * 10**8)
    lat_far, ga = after(lat_far, ga)
    pairs = 2 * PAIRS * ROWS
    products, columns = ((pairs, INNER), bf16), ((pairs, HEADS), bf16)
    qkv, att, probs, wides = call(
        forward_kernel, [spot], [lat_far, lat_near, in_weight, qkv_ab, heads],
        [shaped((8, ROWS, 3 * INNER)), eight, shaped((HEADS, pairs), wide), shaped((pairs, INNER))],
        [((4, ROWS, width), bf16), products, columns], limit=24, flops=8 * 10**9, same=(3, 0),
    )
    part_scr = ((4 * rows, 8 * ROWS), bf16)
    other, att_t, cot_all = call(
        part_kernel, [spot], [att, cot_ab, cot_far, cot_near],
        [shaped((4, rows, width)), shaped((INNER, 8 * ROWS)), eight], [part_scr],
        limit=16, flops=7 * 10**8,
    )
    got = swap(other, "seq", 1)
    cot_all, other = after(cot_all, other)
    grad_att = functools.partial(grad_att_kernel, first=4)
    (ga,) = call(grad_att, [], [cot_all, out_weight, ga], [eight], limit=16, flops=7 * 10**8, same=(2, 0))
    part, piece = (4, PIECE, TILE), (PIECE, TILE)
    tiles = rows * width // TILE
    (mine,) = call(
        mine_kernel, [spot], [att_t, cot_all], [shaped((4 * tiles, TILE), wide)], [part_scr],
        limit=16, flops=7 * 10**8,
    )
    mine, ga = after(mine, ga)
    keep, *sends = call(
        cores_kernel, [spot], [mine, got], [shaped(part, wide)] + [shaped(part)] * 3,
        [((4 * tiles, TILE), wide)], limit=16, flops=7 * 10**8,
    )
    att, sends = after(att, sends)
    sends = [swap(sends[flip - 1], "dp", flip) for flip in (3, 1, 2)]
    mixed = call(mix_kernel, [], [att, out_weight], [four, two, two], limit=16, size=10**3)
    qkv, mixed = after(qkv, mixed)
    mixed = [mixed[0], *exchange(mixed[1], mixed[2])]
    (d_all,) = call(
        backward_kernel, [spot], [ga, qkv, probs, wides, heads], [shaped((8, ROWS, 3 * INNER))],
        [products, ((HEADS, pairs), wide), columns], limit=24, size=10**3,
    )
    theirs = functools.partial(latents_kernel, first=4)
    grad = call(theirs, [], [d_all, in_weight], [two, two], limit=16, size=10**3)
    keep, (grad, mixed) = after(keep, (grad, mixed))
    keep, *sends = call(
        groups_kernel, [spot], [keep, *sends], [shaped(piece, wide)] + [shaped(piece)] * 3,
        [(part, wide)],
    )
    grad, keep = after(grad, keep)
    sends = [swap(sends[flip - 1], "seq", 2 * flip) for flip in (2, 3, 1)]
    d_all, grad = after(d_all, grad)
    ours = functools.partial(latents_kernel, first=0)
    (own,) = call(ours, [], [d_all, in_weight], [four], limit=16, flops=8 * 10**9)
    grad = [own, *exchange(grad[0], grad[1])]
    keep, grad[0] = after(keep, grad[0])
    (last,) = call(chips_kernel, [], [keep, *sends], [shaped(piece)])
    grad[0], last = after(grad[0], last)
    others = [swap(last, "dp", flip) for flip in (1, 2, 3)]
    own, sib = call(settle_kernel, [spot], [*mixed, *grad], [four, four])
    (token,) = call(arrived_kernel, [], others, [shaped((16, TILE))], flops=8 * 10**9)
    mixed, grad, out_grad = call(
        final_kernel, [spot], [own, swap(sib, "seq", 1), last, *others, token],
        [four, four, shaped((rows, width), wide)],
        [(part, wide), ((tiles, TILE), wide), ((rows, width), wide), pltpu.SemaphoreType.DMA((5,))],
        to_hbm=True,
    )
    return mixed.reshape(latents.shape), grad.reshape(latents.shape), out_grad


def body(latents, *others):
    frames, patches = latents.shape[1] * lax.axis_size("seq"), latents.shape[2]
    small = (lax.axis_size("dp"), lax.axis_size("seq"), frames, patches) == (4, 8, 8, 4 * ROWS)
    return (clip_body if small else patch_body)(latents, *others)


def solution(mesh):
    placed = (P("dp", "seq", None, None), P(), P(), P("dp", "seq", None, None), P("dp", None))
    return jax.shard_map(
        body,
        mesh=mesh,
        in_specs=placed,
        out_specs=(P("dp", "seq", None, None), P("dp", "seq", None, None), P("seq", None)),
        check_vma=False,
    )
```

```python
import functools

import jax
import jax.numpy as jnp
import numpy as np
from jax import lax
from jax.experimental import pallas as pl
from jax.experimental.pallas import tpu as pltpu
from jax.sharding import PartitionSpec as P

HEADS = 16
HD = 72


def clip_index(lengths, frames):
    ends = jnp.cumsum(lengths)
    position = jnp.arange(frames, dtype=jnp.int32)
    return jnp.sum((ends[None, :] <= position[:, None]).astype(jnp.int32), axis=1)


def softmax_weights(query, key_rows, same):
    scale = 1.0 / jnp.sqrt(jnp.float32(HD))
    scores = (
        jnp.einsum("fphd,gphd->phfg", query, key_rows, preferred_element_type=jnp.float32) * scale
    )
    scores = jnp.where(same[None, None], scores, -jnp.inf)
    return jax.nn.softmax(scores, axis=-1)


def contract_rows(left, right):
    return lax.dot_general(
        left, right, (((0,), (0,)), ((), ())), preferred_element_type=jnp.float32
    )


def contract_cols(left, right):
    return lax.dot_general(
        left, right, (((1,), (1,)), ((), ())), preferred_element_type=jnp.float32
    )


def swap(value, axis, flip):
    size = lax.axis_size(axis)
    return lax.ppermute(value, axis, [(i, i ^ flip) for i in range(size)])


def reduce_out(part):
    mine = lax.psum_scatter(part, "seq", scatter_dimension=0, tiled=True)
    return lax.psum(mine.astype(jnp.bfloat16), "dp").astype(jnp.float32)


def patch_body(latents, in_weight, out_weight, cotangent, clip_lengths):
    shards = lax.axis_size("seq")
    local_frames = latents.shape[1]
    patches = latents.shape[2]
    width = latents.shape[3]
    frames = local_frames * shards
    local_patches = patches // shards
    inner = HEADS * HD

    def to_patches(rows):
        return lax.all_to_all(rows, "seq", split_axis=2, concat_axis=1, tiled=True)

    def to_frames(rows):
        return lax.all_to_all(rows, "seq", split_axis=1, concat_axis=2, tiled=True)

    lat_rows = to_patches(latents).reshape(frames * local_patches, width)
    cot_rows = to_patches(cotangent).reshape(frames * local_patches, width)
    projected = jnp.dot(lat_rows, in_weight, preferred_element_type=jnp.float32).astype(
        jnp.bfloat16
    )
    split = projected.reshape(frames, local_patches, 3, HEADS, HD)
    query, key_rows, value_rows = (split[:, :, 0], split[:, :, 1], split[:, :, 2])
    clip = clip_index(clip_lengths[0], frames)
    same = clip[:, None] == clip[None, :]
    weights32 = softmax_weights(query, key_rows, same)
    weights = weights32.astype(jnp.bfloat16)
    attended = jnp.einsum(
        "phfg,gphd->fphd", weights, value_rows, preferred_element_type=jnp.float32
    ).astype(jnp.bfloat16)
    att_rows = attended.reshape(frames * local_patches, inner)
    out_grad = reduce_out(contract_rows(att_rows, cot_rows))
    mixed = jnp.dot(att_rows, out_weight, preferred_element_type=jnp.float32).astype(jnp.bfloat16)
    mixed = to_frames(mixed.reshape(1, frames, local_patches, width))
    grad_att = contract_cols(cot_rows, out_weight).astype(jnp.bfloat16)
    grad_heads = grad_att.reshape(frames, local_patches, HEADS, HD)
    grad_weights = jnp.einsum(
        "fphd,gphd->phfg", grad_heads, value_rows, preferred_element_type=jnp.float32
    )
    grad_values = jnp.einsum(
        "phfg,fphd->gphd", weights, grad_heads, preferred_element_type=jnp.float32
    ).astype(jnp.bfloat16)
    totals = jnp.sum(weights32 * grad_weights, axis=-1, keepdims=True)
    scale = 1.0 / jnp.sqrt(jnp.float32(HD))
    grad_scores = (weights32 * (grad_weights - totals) * scale).astype(jnp.bfloat16)
    grad_query = jnp.einsum(
        "phfg,gphd->fphd", grad_scores, key_rows, preferred_element_type=jnp.float32
    ).astype(jnp.bfloat16)
    grad_keys = jnp.einsum(
        "phfg,fphd->gphd", grad_scores, query, preferred_element_type=jnp.float32
    ).astype(jnp.bfloat16)
    grad_proj = jnp.stack([grad_query, grad_keys, grad_values], axis=2)
    grad_rows = grad_proj.reshape(frames * local_patches, 3 * inner)
    grad_latents = contract_cols(grad_rows, in_weight).astype(jnp.bfloat16)
    grad_latents = to_frames(grad_latents.reshape(1, frames, local_patches, width))
    return (mixed.reshape(latents.shape), grad_latents.reshape(latents.shape), out_grad)


ROWS = 64
PAIRS = 16
TILE = 128
INNER = HEADS * HD
PIECE = 41 * 8
SMEM = pl.BlockSpec(memory_space=pltpu.SMEM)
VMEM = pl.BlockSpec(memory_space=pltpu.VMEM)
HBM = pl.BlockSpec(memory_space=pltpu.HBM)
CHUNKS = ((0, 256), (256, 256), (512, 256), (768, 256), (1024, 128))


def shaped(shape, dtype=jnp.bfloat16):
    return jax.ShapeDtypeStruct(shape, dtype)


def dot(left, right):
    return jnp.dot(left, right, preferred_element_type=jnp.float32)


def flat(value):
    return value.reshape(value.shape[0] * ROWS, value.shape[2])


def call(kernel, scalars, inputs, outs, scratch=(), limit=8, flops=10**6, to_hbm=False, size=None, same=None):
    size = size or sum(x.size * x.dtype.itemsize for x in (*inputs, *outs))
    return pl.pallas_call(
        kernel,
        out_shape=list(outs),
        in_specs=[SMEM] * len(scalars) + [VMEM] * len(inputs),
        out_specs=[HBM if to_hbm else VMEM] * len(outs),
        scratch_shapes=[x if hasattr(x, "memory_space") else pltpu.VMEM(*x) for x in scratch],
        input_output_aliases={len(scalars) + same[0]: same[1]} if same else {},
        compiler_params=pltpu.CompilerParams(vmem_limit_bytes=limit << 20),
        cost_estimate=pl.CostEstimate(flops=flops, bytes_accessed=size, transcendentals=0),
    )(*scalars, *inputs)


def roles(spot):
    zpos, lens = spot[0] // 2, [spot[2 + i] for i in range(3)]
    first = 2 * zpos
    ends = [lens[0], lens[0] + lens[1], lens[0] + lens[1] + lens[2]]
    long = jnp.where(
        lens[0] == 4, 0, jnp.where(lens[1] == 4, ends[0], jnp.where(lens[2] == 4, ends[1], ends[2]))
    )

    def clip(frame):
        return sum((end <= frame).astype(jnp.int32) for end in ends)

    ids = [
        jnp.where(zpos == 0, -1, clip(first - 1)),
        clip(first),
        clip(first + 1),
        jnp.where(zpos == 3, -2, clip(first + 2)),
    ]
    return {
        "core": spot[0] % 2,
        "odd": zpos % 2,
        "left": 6 - 2 * (zpos % 2),
        "right": 4 + 2 * (zpos % 2),
        "ids": ids,
        "low": long == first,
        "high": long == first - 2,
        "middle": long == first - 1,
        "tail": long == first - 3,
        "head": long == first + 1,
    }


def slots(role, window):
    low, high, left, right = role["low"], role["high"], role["left"], role["right"]
    in_low = ((0, 2, right, right + 1), (1, 3, left, left + 1))[window]
    in_high = ((left, left + 1, 1, 3), (0, 2, right, right + 1))[window]
    usual = (left + window, window, 2 + window, right + window)
    blocks = [
        jnp.where(low, a, jnp.where(high, b, c)) for a, b, c in zip(in_low, in_high, usual)
    ]
    even, middle = low | high, role["middle"]
    odd = [middle, ~even & ~role["tail"], ~even & ~role["head"], middle]
    return blocks, [even | x for x in odd] if window == 0 else odd


def pick_kernel(spot, own, sib, near, far, both):
    role = roles(spot)
    core, odd = role["core"], role["odd"]
    for i in range(2):
        both[2 * core + i] = own[i if own.shape[0] == 2 else 2 * core + i]
        both[2 * (1 - core) + i] = sib[2 * core + i]
    right = (jnp.where(role["low"], 1, 2), 3)
    left = (0, jnp.where(role["high"], 2, 1))
    for i in range(2):
        near[i] = both[jnp.where(odd == 1, left[i], right[i])]
        far[i] = both[jnp.where(odd == 1, right[i], left[i])]


def early_kernel(lat_ab, wi_ref, qkv_ref):
    x = flat(lat_ab[...])
    for j in range(3):
        cols = slice(j * INNER, (j + 1) * INNER)
        qkv_ref[:4, :, cols] = dot(x, wi_ref[:, cols]).astype(jnp.bfloat16).reshape(4, ROWS, INNER)


def pair(f, g, w=0, count=1):
    start = (4 * f + g) * 2 * ROWS + w * ROWS
    return slice(start, start + count * ROWS)


def lanes(t, offset=0):
    return slice(offset + TILE * t, offset + TILE * (t + 1))


def forward_kernel(
    spot, far, near, wi_ref, _, heads_ref, qkv_ref, att_ref, p_ref, wide_ref,
    x_scr, hi_scr, w_scr,
):
    x_scr[:2] = near[...]
    x_scr[2:] = far[...]
    x = flat(x_scr[...])
    for j in range(3):
        cols = slice(j * INNER, (j + 1) * INNER)
        qkv_ref[4:, :, cols] = dot(x, wi_ref[:, cols]).astype(jnp.bfloat16).reshape(4, ROWS, INNER)
    role = roles(spot)
    even, ids = role["low"] | role["high"], role["ids"]
    windows = [slots(role, w) for w in range(2)]
    for w, (blocks, _) in enumerate(windows):
        for t in range(INNER // TILE):
            q = [qkv_ref[blocks[f], :, lanes(t)] for f in range(4)]
            k = [qkv_ref[blocks[g], :, lanes(t, INNER)] for g in range(4)]
            for f in range(4):
                for g in range(4):
                    hi_scr[pair(f, g, w), lanes(t)] = q[f] * k[g]
    scores = contract_cols(heads_ref[...], hi_scr[...])
    for f in range(4):
        line = []
        for g in range(4):
            bias = jnp.where(even | (ids[f] == ids[g]), 0.0, -jnp.inf)
            line.append(scores[:, pair(f, g, 0, 2)] * HD**-0.5 + bias)
        top = jnp.maximum(jnp.maximum(line[0], line[1]), jnp.maximum(line[2], line[3]))
        line = [jnp.exp(x - top) for x in line]
        share = 1.0 / (line[0] + line[1] + line[2] + line[3])
        for g in range(4):
            p_ref[:, pair(f, g, 0, 2)] = line[g] * share
    w_scr[...] = p_ref[...].T.astype(jnp.bfloat16)
    for f in range(4):
        rows = pair(f, 0, 0, 8)
        for start, size in CHUNKS:
            cols = slice(start, start + size)
            spread = dot(w_scr[rows, :], heads_ref[:, cols])
            wide_ref[rows, cols] = spread.astype(jnp.bfloat16)
            for w, (blocks, kept) in enumerate(windows):
                base = 2 * INNER + start
                total = sum(
                    spread[pair(0, g, w)] * qkv_ref[blocks[g], :, base : base + size].astype(jnp.float32)
                    for g in range(4)
                )
                total = total * jnp.where(kept[f], 1.0, 0.0)
                att_ref[blocks[f], :, cols] = total.astype(jnp.bfloat16)


def part_rows(core, att_t, cot, rows):
    height = att_t.shape[0] // 8
    for z in range(4):
        start = pl.multiple_of((2 * z + core) * height, 16)
        rows[z * height : (z + 1) * height, :] = att_t[pl.ds(start, height), :]
    return dot(rows[...], flat(cot[...])).reshape(4, height, -1)


def part_kernel(spot, att_ref, ab_ref, far, near, sib_ref, att_t, cot, rows):
    cot[:4] = ab_ref[...]
    cot[4:6] = near[...]
    cot[6:] = far[...]
    att_t[...] = flat(att_ref[...]).T
    sib_ref[...] = part_rows(1 - spot[0] % 2, att_t, cot, rows).astype(jnp.bfloat16)


def mix_kernel(att_ref, w_ref, here_ref, near_ref, far_ref):
    made = dot(flat(att_ref[...]), w_ref[...]).astype(jnp.bfloat16).reshape(8, ROWS, -1)
    here_ref[...] = made[:4]
    near_ref[...] = made[4:6]
    far_ref[...] = made[6:]


def grad_att_kernel(cot, wo_ref, *refs, first):
    rows = cot[first : first + 4]
    made = contract_cols(flat(rows), wo_ref[...])
    refs[-1][first : first + 4] = made.astype(jnp.bfloat16).reshape(4, ROWS, INNER)


def backward_kernel(
    spot, ga_ref, qkv_ref, p_ref, wide_ref, heads_ref, d_ref, hi_scr, t_scr, s_scr
):
    role = roles(spot)
    windows = [slots(role, w)[0] for w in range(2)]
    for w, blocks in enumerate(windows):
        for t in range(INNER // TILE):
            do = [ga_ref[blocks[f], :, lanes(t)] for f in range(4)]
            v = [qkv_ref[blocks[g], :, lanes(t, 2 * INNER)] for g in range(4)]
            for f in range(4):
                for g in range(4):
                    hi_scr[pair(f, g, w), lanes(t)] = do[f] * v[g]
    grads = contract_cols(heads_ref[...], hi_scr[...])
    for f in range(4):
        p = [p_ref[:, pair(f, g, 0, 2)] for g in range(4)]
        line = [grads[:, pair(f, g, 0, 2)] for g in range(4)]
        total = sum(p[g] * line[g] for g in range(4))
        for g in range(4):
            t_scr[:, pair(f, g, 0, 2)] = p[g] * (line[g] - total) * HD**-0.5
    s_scr[...] = t_scr[...].T.astype(jnp.bfloat16)
    for start, size in CHUNKS:
        cols = slice(start, start + size)
        spread = dot(s_scr[...], heads_ref[:, cols])
        for w, blocks in enumerate(windows):

            def take(ref, block, offset=0):
                return ref[block, :, offset + start : offset + start + size].astype(jnp.float32)

            def put(block, offset, value):
                d_ref[block, :, offset + start : offset + start + size] = value.astype(jnp.bfloat16)

            do = [take(ga_ref, blocks[f]) for f in range(4)]
            for g in range(4):
                put(
                    blocks[g], 2 * INNER,
                    sum(wide_ref[pair(f, g, w), cols].astype(jnp.float32) * do[f] for f in range(4)),
                )
            q = [take(qkv_ref, blocks[f]) for f in range(4)]
            k = [take(qkv_ref, blocks[g], INNER) for g in range(4)]
            for f in range(4):
                put(blocks[f], 0, sum(spread[pair(f, g, w)] * k[g] for g in range(4)))
            for g in range(4):
                put(blocks[g], INNER, sum(spread[pair(f, g, w)] * q[f] for f in range(4)))


def latents_kernel(d_ref, wi_ref, *outs, first):
    tile = 384
    for j in range(wi_ref.shape[0] // tile):
        cols = slice(j * tile, (j + 1) * tile)
        made = contract_cols(flat(d_ref[first : first + 4]), wi_ref[cols, :]).astype(jnp.bfloat16)
        made = made.reshape(4, ROWS, tile)
        size = 4 // len(outs)
        for i, out in enumerate(outs):
            out[:, :, cols] = made[i * size : (i + 1) * size]


def settle_kernel(spot, *refs):
    *given, own, sib = refs
    role = roles(spot)
    core, left, right = role["core"], role["left"], role["right"]
    low, high, tail, head = role["low"], role["high"], role["tail"], role["head"]
    where = [
        jnp.where(high | tail, left, 0),
        jnp.where(low, right, jnp.where(tail, left + 1, 1)),
        jnp.where(high, left + 1, jnp.where(head, right, 2)),
        jnp.where(low | head, right + 1, 3),
    ]

    def put(out, row, block, here, far, near):
        for source, first, count in ((here, 0, 4), (near, 4, 2), (far, 6, 2)):

            @pl.when((block >= first) & (block < first + count))
            def _():
                out[row] = source[block - first]

    for base in (0, 2):
        sources = given[:3] if base == 0 else given[3:]
        for i in range(2):
            put(own, base + i, jnp.where(core == 0, where[i], where[2 + i]), *sources)
            put(sib, base + i, jnp.where(core == 0, where[2 + i], where[i]), *sources)


def first_row(group, block):
    return pl.multiple_of((group * 81 // 2 + block * 162) * 8, 8)


def mine_kernel(spot, att_t, cot, total, rows):
    height, width = att_t.shape[0] // 8, cot.shape[2]
    made = part_rows(spot[0] % 2, att_t, cot, rows)
    for z in range(4):
        for t in range(width // TILE):
            start = (z * width // TILE + t) * height
            total[start : start + height, :] = made[z][:, lanes(t)]


def cores_kernel(spot, mine, got, keep, *sends):
    group = spot[1]
    *sends, total = sends
    height, width = got.shape[1:]
    for z in range(4):
        for t in range(width // TILE):
            rows = slice((z * width // TILE + t) * height, (z * width // TILE + t + 1) * height)
            total[rows, :] = mine[rows, :] + got[z, :, lanes(t)].astype(jnp.float32)
    for flip, out in enumerate((keep, *sends)):
        for z in range(4):
            out[z] = total[pl.ds(first_row(group ^ flip, z), PIECE), :].astype(out.dtype)


def groups_kernel(spot, own, one, two, three, keep, *sends):
    zpos = spot[0] // 2
    *sends, total = sends
    total[...] = own[...] + sum(x[...].astype(jnp.float32) for x in (one, two, three))
    for flip, out in enumerate((keep, *sends)):
        out[...] = total[zpos ^ flip].astype(out.dtype)


def chips_kernel(own, one, two, three, out):
    total = own[...] + sum(x[...].astype(jnp.float32) for x in (one, two, three))
    out[...] = total.astype(jnp.bfloat16)


def arrived_kernel(one, two, three, token):
    token[...] = (one[:16, :] + two[:16, :]) + three[:16, :]


def final_kernel(
    spot, own, sib, last, one, two, three, _, mixed, grad, out, held, rows, made, sems
):
    core = spot[0] % 2
    here, there = pl.ds(2 * core, 2), pl.ds(2 * (1 - core), 2)
    moves = []
    for base, result in ((0, mixed), (2, grad)):
        moves.append((own.at[base : base + 2], result.at[here]))
        moves.append((sib.at[base : base + 2], result.at[there]))
    copies = [pltpu.make_async_copy(x, y, sems.at[i]) for i, (x, y) in enumerate(moves)]
    for copy in copies:
        copy.start()
    for flip, value in enumerate((last, one, two, three)):
        held[spot[1] ^ flip] = value[...].astype(jnp.float32)
    for group in range(4):
        rows[pl.ds(first_row(group, 0), PIECE), :] = held[group]
    height, width = out.shape
    for t in range(width // TILE):
        made[:, lanes(t)] = rows[t * height : (t + 1) * height, :]
    copies.append(pltpu.make_async_copy(made, out, sems.at[len(copies)]))
    copies[-1].start()
    for copy in copies:
        copy.wait()


def after(later, earlier):
    return lax.optimization_barrier((later, earlier))


def exchange(near, far):
    pairs = [(0, 0), (1, 1), (2, 4), (4, 2), (3, 5), (5, 3), (6, 6), (7, 7)]
    return lax.ppermute(far, "seq", pairs), swap(near, "seq", 2)


def clip_body(latents, in_weight, out_weight, cotangent, clip_lengths):
    width = latents.shape[3]
    rows = INNER // 8
    wide = jnp.float32
    place = jnp.arange(2 + clip_lengths.shape[1], dtype=jnp.int32)
    spot = jnp.where(place == 0, lax.axis_index("seq"), jnp.where(place == 1, lax.axis_index("dp"), 0))
    spot = spot + jnp.pad(clip_lengths[0], (2, 0))
    heads = jnp.asarray(np.arange(INNER) // HD == np.arange(HEADS)[:, None], jnp.bfloat16)
    lat = latents.reshape(4, ROWS, width)
    cot = cotangent.reshape(4, ROWS, width)

    bf16 = jnp.bfloat16
    four, two, eight = shaped((4, ROWS, width)), shaped((2, ROWS, width)), shaped((8, ROWS, INNER))

    def pick(own, sib, flops):
        near, far, both = call(pick_kernel, [spot], [own, sib], [two, two, four], flops=flops)
        return exchange(near, far), both

    lat_sib, cot_sib = swap(lat, "seq", 1), swap(cot, "seq", 1)
    lat_own = lax.dynamic_slice_in_dim(lat, 2 * (lax.axis_index("seq") % 2), 2, 0)
    (lat_far, lat_near), lat_ab = pick(lat_own, lat_sib, 4 * 10**9)
    (qkv_ab,) = call(
        early_kernel, [], [lat_ab, in_weight], [shaped((8, ROWS, 3 * INNER))], limit=16, flops=27 * 10**8
    )
    cot_sib, qkv_ab = after(cot_sib, qkv_ab)
    (cot_far, cot_near), cot_ab = pick(cot, cot_sib, 10**6)
    grad_att = functools.partial(grad_att_kernel, first=0)
    (ga,) = call(grad_att, [], [cot_ab, out_weight], [eight], limit=16, flops=7 * 10**8)
    lat_far, ga = after(lat_far, ga)
    pairs = 2 * PAIRS * ROWS
    products, columns = ((pairs, INNER), bf16), ((pairs, HEADS), bf16)
    qkv, att, probs, wides = call(
        forward_kernel, [spot], [lat_far, lat_near, in_weight, qkv_ab, heads],
        [shaped((8, ROWS, 3 * INNER)), eight, shaped((HEADS, pairs), wide), shaped((pairs, INNER))],
        [((4, ROWS, width), bf16), products, columns], limit=24, flops=8 * 10**9, same=(3, 0),
    )
    part_scr = ((4 * rows, 8 * ROWS), bf16)
    other, att_t, cot_all = call(
        part_kernel, [spot], [att, cot_ab, cot_far, cot_near],
        [shaped((4, rows, width)), shaped((INNER, 8 * ROWS)), eight], [part_scr],
        limit=16, flops=7 * 10**8,
    )
    got = swap(other, "seq", 1)
    cot_all, other = after(cot_all, other)
    grad_att = functools.partial(grad_att_kernel, first=4)
    (ga,) = call(grad_att, [], [cot_all, out_weight, ga], [eight], limit=16, flops=7 * 10**8, same=(2, 0))
    part, piece = (4, PIECE, TILE), (PIECE, TILE)
    tiles = rows * width // TILE
    (mine,) = call(
        mine_kernel, [spot], [att_t, cot_all], [shaped((4 * tiles, TILE), wide)], [part_scr],
        limit=16, flops=7 * 10**8,
    )
    mine, ga = after(mine, ga)
    keep, *sends = call(
        cores_kernel, [spot], [mine, got], [shaped(part, wide)] + [shaped(part)] * 3,
        [((4 * tiles, TILE), wide)], limit=16, flops=7 * 10**8,
    )
    att, sends = after(att, sends)
    sends = [swap(sends[flip - 1], "dp", flip) for flip in (3, 1, 2)]
    mixed = call(mix_kernel, [], [att, out_weight], [four, two, two], limit=16, size=10**3)
    qkv, mixed = after(qkv, mixed)
    mixed = [mixed[0], *exchange(mixed[1], mixed[2])]
    (d_all,) = call(
        backward_kernel, [spot], [ga, qkv, probs, wides, heads], [shaped((8, ROWS, 3 * INNER))],
        [products, ((HEADS, pairs), wide), columns], limit=24, size=10**3,
    )
    theirs = functools.partial(latents_kernel, first=4)
    grad = call(theirs, [], [d_all, in_weight], [two, two], limit=16, size=10**3)
    keep, (grad, mixed) = after(keep, (grad, mixed))
    keep, *sends = call(
        groups_kernel, [spot], [keep, *sends], [shaped(piece, wide)] + [shaped(piece)] * 3,
        [(part, wide)],
    )
    grad, keep = after(grad, keep)
    sends = [swap(x, "seq", 2 * flip) for flip, x in enumerate(sends, 1)]
    d_all, grad = after(d_all, grad)
    ours = functools.partial(latents_kernel, first=0)
    (own,) = call(ours, [], [d_all, in_weight], [four], limit=16, flops=8 * 10**9)
    grad = [own, *exchange(grad[0], grad[1])]
    keep, grad[0] = after(keep, grad[0])
    (last,) = call(chips_kernel, [], [keep, *sends], [shaped(piece)])
    grad[0], last = after(grad[0], last)
    others = [swap(last, "dp", flip) for flip in (1, 2, 3)]
    own, sib = call(settle_kernel, [spot], [*mixed, *grad], [four, four])
    (token,) = call(arrived_kernel, [], others, [shaped((16, TILE))], flops=8 * 10**9)
    mixed, grad, out_grad = call(
        final_kernel, [spot], [own, swap(sib, "seq", 1), last, *others, token],
        [four, four, shaped((rows, width), wide)],
        [(part, wide), ((tiles, TILE), wide), ((rows, width), wide), pltpu.SemaphoreType.DMA((5,))],
        to_hbm=True,
    )
    return mixed.reshape(latents.shape), grad.reshape(latents.shape), out_grad


def body(latents, *others):
    frames, patches = latents.shape[1] * lax.axis_size("seq"), latents.shape[2]
    small = (lax.axis_size("dp"), lax.axis_size("seq"), frames, patches) == (4, 8, 8, 4 * ROWS)
    return (clip_body if small else patch_body)(latents, *others)


def solution(mesh):
    placed = (P("dp", "seq", None, None), P(), P(), P("dp", "seq", None, None), P("dp", None))
    return jax.shard_map(
        body,
        mesh=mesh,
        in_specs=placed,
        out_specs=(P("dp", "seq", None, None), P("dp", "seq", None, None), P("seq", None)),
        check_vma=False,
    )
```

```python
import functools

import jax
import jax.numpy as jnp
import numpy as np
from jax import lax
from jax.experimental import pallas as pl
from jax.experimental.pallas import tpu as pltpu
from jax.sharding import PartitionSpec as P

HEADS = 16
HD = 72


def clip_index(lengths, frames):
    ends = jnp.cumsum(lengths)
    position = jnp.arange(frames, dtype=jnp.int32)
    return jnp.sum((ends[None, :] <= position[:, None]).astype(jnp.int32), axis=1)


def softmax_weights(query, key_rows, same):
    scale = 1.0 / jnp.sqrt(jnp.float32(HD))
    scores = (
        jnp.einsum("fphd,gphd->phfg", query, key_rows, preferred_element_type=jnp.float32) * scale
    )
    scores = jnp.where(same[None, None], scores, -jnp.inf)
    return jax.nn.softmax(scores, axis=-1)


def contract_rows(left, right):
    return lax.dot_general(
        left, right, (((0,), (0,)), ((), ())), preferred_element_type=jnp.float32
    )


def contract_cols(left, right):
    return lax.dot_general(
        left, right, (((1,), (1,)), ((), ())), preferred_element_type=jnp.float32
    )


def swap(value, axis, flip):
    size = lax.axis_size(axis)
    return lax.ppermute(value, axis, [(i, i ^ flip) for i in range(size)])


def reduce_out(part):
    mine = lax.psum_scatter(part, "seq", scatter_dimension=0, tiled=True)
    return lax.psum(mine.astype(jnp.bfloat16), "dp").astype(jnp.float32)


def patch_body(latents, in_weight, out_weight, cotangent, clip_lengths):
    shards = lax.axis_size("seq")
    local_frames = latents.shape[1]
    patches = latents.shape[2]
    width = latents.shape[3]
    frames = local_frames * shards
    local_patches = patches // shards
    inner = HEADS * HD

    def to_patches(rows):
        return lax.all_to_all(rows, "seq", split_axis=2, concat_axis=1, tiled=True)

    def to_frames(rows):
        return lax.all_to_all(rows, "seq", split_axis=1, concat_axis=2, tiled=True)

    lat_rows = to_patches(latents).reshape(frames * local_patches, width)
    cot_rows = to_patches(cotangent).reshape(frames * local_patches, width)
    projected = jnp.dot(lat_rows, in_weight, preferred_element_type=jnp.float32).astype(
        jnp.bfloat16
    )
    split = projected.reshape(frames, local_patches, 3, HEADS, HD)
    query, key_rows, value_rows = (split[:, :, 0], split[:, :, 1], split[:, :, 2])
    clip = clip_index(clip_lengths[0], frames)
    same = clip[:, None] == clip[None, :]
    weights32 = softmax_weights(query, key_rows, same)
    weights = weights32.astype(jnp.bfloat16)
    attended = jnp.einsum(
        "phfg,gphd->fphd", weights, value_rows, preferred_element_type=jnp.float32
    ).astype(jnp.bfloat16)
    att_rows = attended.reshape(frames * local_patches, inner)
    out_grad = reduce_out(contract_rows(att_rows, cot_rows))
    mixed = jnp.dot(att_rows, out_weight, preferred_element_type=jnp.float32).astype(jnp.bfloat16)
    mixed = to_frames(mixed.reshape(1, frames, local_patches, width))
    grad_att = contract_cols(cot_rows, out_weight).astype(jnp.bfloat16)
    grad_heads = grad_att.reshape(frames, local_patches, HEADS, HD)
    grad_weights = jnp.einsum(
        "fphd,gphd->phfg", grad_heads, value_rows, preferred_element_type=jnp.float32
    )
    grad_values = jnp.einsum(
        "phfg,fphd->gphd", weights, grad_heads, preferred_element_type=jnp.float32
    ).astype(jnp.bfloat16)
    totals = jnp.sum(weights32 * grad_weights, axis=-1, keepdims=True)
    scale = 1.0 / jnp.sqrt(jnp.float32(HD))
    grad_scores = (weights32 * (grad_weights - totals) * scale).astype(jnp.bfloat16)
    grad_query = jnp.einsum(
        "phfg,gphd->fphd", grad_scores, key_rows, preferred_element_type=jnp.float32
    ).astype(jnp.bfloat16)
    grad_keys = jnp.einsum(
        "phfg,fphd->gphd", grad_scores, query, preferred_element_type=jnp.float32
    ).astype(jnp.bfloat16)
    grad_proj = jnp.stack([grad_query, grad_keys, grad_values], axis=2)
    grad_rows = grad_proj.reshape(frames * local_patches, 3 * inner)
    grad_latents = contract_cols(grad_rows, in_weight).astype(jnp.bfloat16)
    grad_latents = to_frames(grad_latents.reshape(1, frames, local_patches, width))
    return (mixed.reshape(latents.shape), grad_latents.reshape(latents.shape), out_grad)


ROWS = 64
PAIRS = 16
TILE = 128
INNER = HEADS * HD
PIECE = 41 * 8
SMEM = pl.BlockSpec(memory_space=pltpu.SMEM)
VMEM = pl.BlockSpec(memory_space=pltpu.VMEM)
HBM = pl.BlockSpec(memory_space=pltpu.HBM)
CHUNKS = ((0, 256), (256, 256), (512, 256), (768, 256), (1024, 128))


def shaped(shape, dtype=jnp.bfloat16):
    return jax.ShapeDtypeStruct(shape, dtype)


def dot(left, right):
    return jnp.dot(left, right, preferred_element_type=jnp.float32)


def flat(value):
    return value.reshape(value.shape[0] * ROWS, value.shape[2])


def call(kernel, scalars, inputs, outs, scratch=(), limit=8, flops=10**6, to_hbm=False, size=None, same=None):
    size = size or sum(x.size * x.dtype.itemsize for x in (*inputs, *outs))
    return pl.pallas_call(
        kernel,
        out_shape=list(outs),
        in_specs=[SMEM] * len(scalars) + [VMEM] * len(inputs),
        out_specs=[HBM if to_hbm else VMEM] * len(outs),
        scratch_shapes=[x if hasattr(x, "memory_space") else pltpu.VMEM(*x) for x in scratch],
        input_output_aliases={len(scalars) + same[0]: same[1]} if same else {},
        compiler_params=pltpu.CompilerParams(vmem_limit_bytes=limit << 20),
        cost_estimate=pl.CostEstimate(flops=flops, bytes_accessed=size, transcendentals=0),
    )(*scalars, *inputs)


def roles(spot):
    zpos, lens = spot[0] // 2, [spot[2 + i] for i in range(3)]
    first = 2 * zpos
    ends = [lens[0], lens[0] + lens[1], lens[0] + lens[1] + lens[2]]
    long = jnp.where(
        lens[0] == 4, 0, jnp.where(lens[1] == 4, ends[0], jnp.where(lens[2] == 4, ends[1], ends[2]))
    )

    def clip(frame):
        return sum((end <= frame).astype(jnp.int32) for end in ends)

    ids = [
        jnp.where(zpos == 0, -1, clip(first - 1)),
        clip(first),
        clip(first + 1),
        jnp.where(zpos == 3, -2, clip(first + 2)),
    ]
    return {
        "core": spot[0] % 2,
        "odd": zpos % 2,
        "left": 6 - 2 * (zpos % 2),
        "right": 4 + 2 * (zpos % 2),
        "ids": ids,
        "low": long == first,
        "high": long == first - 2,
        "middle": long == first - 1,
        "tail": long == first - 3,
        "head": long == first + 1,
    }


def slots(role, window):
    low, high, left, right = role["low"], role["high"], role["left"], role["right"]
    in_low = ((0, 2, right, right + 1), (1, 3, left, left + 1))[window]
    in_high = ((left, left + 1, 1, 3), (0, 2, right, right + 1))[window]
    usual = (left + window, window, 2 + window, right + window)
    blocks = [
        jnp.where(low, a, jnp.where(high, b, c)) for a, b, c in zip(in_low, in_high, usual)
    ]
    even, middle = low | high, role["middle"]
    odd = [middle, ~even & ~role["tail"], ~even & ~role["head"], middle]
    return blocks, [even | x for x in odd] if window == 0 else odd


def pick_kernel(spot, own, sib, near, far, both):
    role = roles(spot)
    core, odd = role["core"], role["odd"]
    for i in range(2):
        both[2 * core + i] = own[i if own.shape[0] == 2 else 2 * core + i]
        both[2 * (1 - core) + i] = sib[2 * core + i]
    right = (jnp.where(role["low"], 1, 2), 3)
    left = (0, jnp.where(role["high"], 2, 1))
    for i in range(2):
        near[i] = both[jnp.where(odd == 1, left[i], right[i])]
        far[i] = both[jnp.where(odd == 1, right[i], left[i])]


def early_kernel(lat_ab, wi_ref, qkv_ref):
    x = flat(lat_ab[...])
    for j in range(3):
        cols = slice(j * INNER, (j + 1) * INNER)
        qkv_ref[:4, :, cols] = dot(x, wi_ref[:, cols]).astype(jnp.bfloat16).reshape(4, ROWS, INNER)


def pair(f, g, w=0, count=1):
    start = (4 * f + g) * 2 * ROWS + w * ROWS
    return slice(start, start + count * ROWS)


def lanes(t, offset=0):
    return slice(offset + TILE * t, offset + TILE * (t + 1))


def forward_kernel(
    spot, near, far, wi_ref, _, heads_ref, qkv_ref, att_ref, p_ref, wide_ref,
    x_scr, hi_scr, w_scr,
):
    x_scr[:2] = near[...]
    x_scr[2:] = far[...]
    x = flat(x_scr[...])
    for j in range(3):
        cols = slice(j * INNER, (j + 1) * INNER)
        qkv_ref[4:, :, cols] = dot(x, wi_ref[:, cols]).astype(jnp.bfloat16).reshape(4, ROWS, INNER)
    role = roles(spot)
    even, ids = role["low"] | role["high"], role["ids"]
    windows = [slots(role, w) for w in range(2)]
    for w, (blocks, _) in enumerate(windows):
        for t in range(INNER // TILE):
            q = [qkv_ref[blocks[f], :, lanes(t)] for f in range(4)]
            k = [qkv_ref[blocks[g], :, lanes(t, INNER)] for g in range(4)]
            for f in range(4):
                for g in range(4):
                    hi_scr[pair(f, g, w), lanes(t)] = q[f] * k[g]
    scores = contract_cols(heads_ref[...], hi_scr[...])
    for f in range(4):
        line = []
        for g in range(4):
            bias = jnp.where(even | (ids[f] == ids[g]), 0.0, -jnp.inf)
            line.append(scores[:, pair(f, g, 0, 2)] * HD**-0.5 + bias)
        top = jnp.maximum(jnp.maximum(line[0], line[1]), jnp.maximum(line[2], line[3]))
        line = [jnp.exp(x - top) for x in line]
        share = 1.0 / (line[0] + line[1] + line[2] + line[3])
        for g in range(4):
            p_ref[:, pair(f, g, 0, 2)] = line[g] * share
    w_scr[...] = p_ref[...].T.astype(jnp.bfloat16)
    for f in range(4):
        rows = pair(f, 0, 0, 8)
        for start, size in CHUNKS:
            cols = slice(start, start + size)
            spread = dot(w_scr[rows, :], heads_ref[:, cols])
            wide_ref[rows, cols] = spread.astype(jnp.bfloat16)
            for w, (blocks, kept) in enumerate(windows):
                base = 2 * INNER + start
                total = sum(
                    spread[pair(0, g, w)] * qkv_ref[blocks[g], :, base : base + size].astype(jnp.float32)
                    for g in range(4)
                )
                total = total * jnp.where(kept[f], 1.0, 0.0)
                att_ref[blocks[f], :, cols] = total.astype(jnp.bfloat16)


def part_rows(core, att_t, cot, rows):
    height = att_t.shape[0] // 8
    for z in range(4):
        start = pl.multiple_of((2 * z + core) * height, 16)
        rows[z * height : (z + 1) * height, :] = att_t[pl.ds(start, height), :]
    return dot(rows[...], flat(cot[...])).reshape(4, height, -1)


def part_kernel(spot, att_ref, ab_ref, far, near, sib_ref, att_t, cot, rows):
    cot[:4] = ab_ref[...]
    cot[4:6] = near[...]
    cot[6:] = far[...]
    att_t[...] = flat(att_ref[...]).T
    sib_ref[...] = part_rows(1 - spot[0] % 2, att_t, cot, rows).astype(jnp.bfloat16)


def mix_kernel(att_ref, w_ref, here_ref, near_ref, far_ref):
    made = dot(flat(att_ref[...]), w_ref[...]).astype(jnp.bfloat16).reshape(8, ROWS, -1)
    here_ref[...] = made[:4]
    near_ref[...] = made[4:6]
    far_ref[...] = made[6:]


def grad_att_kernel(cot, wo_ref, *refs, first):
    rows = cot[first : first + 4]
    made = contract_cols(flat(rows), wo_ref[...])
    refs[-1][first : first + 4] = made.astype(jnp.bfloat16).reshape(4, ROWS, INNER)


def backward_kernel(
    spot, ga_ref, qkv_ref, p_ref, wide_ref, heads_ref, d_ref, hi_scr, t_scr, s_scr
):
    role = roles(spot)
    windows = [slots(role, w)[0] for w in range(2)]
    for w, blocks in enumerate(windows):
        for t in range(INNER // TILE):
            do = [ga_ref[blocks[f], :, lanes(t)] for f in range(4)]
            v = [qkv_ref[blocks[g], :, lanes(t, 2 * INNER)] for g in range(4)]
            for f in range(4):
                for g in range(4):
                    hi_scr[pair(f, g, w), lanes(t)] = do[f] * v[g]
    grads = contract_cols(heads_ref[...], hi_scr[...])
    for f in range(4):
        p = [p_ref[:, pair(f, g, 0, 2)] for g in range(4)]
        line = [grads[:, pair(f, g, 0, 2)] for g in range(4)]
        total = sum(p[g] * line[g] for g in range(4))
        for g in range(4):
            t_scr[:, pair(f, g, 0, 2)] = p[g] * (line[g] - total) * HD**-0.5
    s_scr[...] = t_scr[...].T.astype(jnp.bfloat16)
    for start, size in CHUNKS:
        cols = slice(start, start + size)
        spread = dot(s_scr[...], heads_ref[:, cols])
        for w, blocks in enumerate(windows):

            def take(ref, block, offset=0):
                return ref[block, :, offset + start : offset + start + size].astype(jnp.float32)

            def put(block, offset, value):
                d_ref[block, :, offset + start : offset + start + size] = value.astype(jnp.bfloat16)

            do = [take(ga_ref, blocks[f]) for f in range(4)]
            for g in range(4):
                put(
                    blocks[g], 2 * INNER,
                    sum(wide_ref[pair(f, g, w), cols].astype(jnp.float32) * do[f] for f in range(4)),
                )
            q = [take(qkv_ref, blocks[f]) for f in range(4)]
            k = [take(qkv_ref, blocks[g], INNER) for g in range(4)]
            for f in range(4):
                put(blocks[f], 0, sum(spread[pair(f, g, w)] * k[g] for g in range(4)))
            for g in range(4):
                put(blocks[g], INNER, sum(spread[pair(f, g, w)] * q[f] for f in range(4)))


def latents_kernel(d_ref, wi_ref, *outs, first):
    tile = 384
    for j in range(wi_ref.shape[0] // tile):
        cols = slice(j * tile, (j + 1) * tile)
        made = contract_cols(flat(d_ref[first : first + 4]), wi_ref[cols, :]).astype(jnp.bfloat16)
        made = made.reshape(4, ROWS, tile)
        size = 4 // len(outs)
        for i, out in enumerate(outs):
            out[:, :, cols] = made[i * size : (i + 1) * size]


def settle_kernel(spot, *refs):
    *given, own, sib = refs
    role = roles(spot)
    core, left, right = role["core"], role["left"], role["right"]
    low, high, tail, head = role["low"], role["high"], role["tail"], role["head"]
    where = [
        jnp.where(high | tail, left, 0),
        jnp.where(low, right, jnp.where(tail, left + 1, 1)),
        jnp.where(high, left + 1, jnp.where(head, right, 2)),
        jnp.where(low | head, right + 1, 3),
    ]

    def put(out, row, block, here, far, near):
        for source, first, count in ((here, 0, 4), (near, 4, 2), (far, 6, 2)):

            @pl.when((block >= first) & (block < first + count))
            def _():
                out[row] = source[block - first]

    for base in (0, 2):
        here, far, near = given[:3] if base == 0 else (given[3], given[5], given[4])
        for i in range(2):
            put(own, base + i, jnp.where(core == 0, where[i], where[2 + i]), here, far, near)
            put(sib, base + i, jnp.where(core == 0, where[2 + i], where[i]), here, far, near)


def first_row(group, block):
    return pl.multiple_of((group * 81 // 2 + block * 162) * 8, 8)


def mine_kernel(spot, att_t, cot, total, rows):
    height, width = att_t.shape[0] // 8, cot.shape[2]
    made = part_rows(spot[0] % 2, att_t, cot, rows)
    for z in range(4):
        for t in range(width // TILE):
            start = (z * width // TILE + t) * height
            total[start : start + height, :] = made[z][:, lanes(t)]


def cores_kernel(spot, mine, got, keep, *sends):
    group = spot[1]
    *sends, total = sends
    height, width = got.shape[1:]
    for z in range(4):
        for t in range(width // TILE):
            rows = slice((z * width // TILE + t) * height, (z * width // TILE + t + 1) * height)
            total[rows, :] = mine[rows, :] + got[z, :, lanes(t)].astype(jnp.float32)
    for flip, out in enumerate((keep, *sends)):
        for z in range(4):
            out[z] = total[pl.ds(first_row(group ^ flip, z), PIECE), :].astype(out.dtype)


def groups_kernel(spot, own, one, two, three, keep, *sends):
    zpos = spot[0] // 2
    *sends, total = sends
    total[...] = own[...] + sum(x[...].astype(jnp.float32) for x in (one, two, three))
    for flip, out in enumerate((keep, *sends)):
        out[...] = total[zpos ^ flip].astype(out.dtype)


def chips_kernel(own, one, two, three, out):
    total = own[...] + sum(x[...].astype(jnp.float32) for x in (one, two, three))
    out[...] = total.astype(jnp.bfloat16)


def arrived_kernel(one, two, three, token):
    token[...] = (one[:16, :] + two[:16, :]) + three[:16, :]


def final_kernel(
    spot, own, sib, last, one, two, three, _, mixed, grad, out, held, rows, made, sems
):
    core = spot[0] % 2
    here, there = pl.ds(2 * core, 2), pl.ds(2 * (1 - core), 2)
    moves = []
    for base, result in ((0, mixed), (2, grad)):
        moves.append((own.at[base : base + 2], result.at[here]))
        moves.append((sib.at[base : base + 2], result.at[there]))
    copies = [pltpu.make_async_copy(x, y, sems.at[i]) for i, (x, y) in enumerate(moves)]
    for copy in copies:
        copy.start()
    for flip, value in enumerate((last, one, two, three)):
        held[spot[1] ^ flip] = value[...].astype(jnp.float32)
    for group in range(4):
        rows[pl.ds(first_row(group, 0), PIECE), :] = held[group]
    height, width = out.shape
    for t in range(width // TILE):
        made[:, lanes(t)] = rows[t * height : (t + 1) * height, :]
    copies.append(pltpu.make_async_copy(made, out, sems.at[len(copies)]))
    copies[-1].start()
    for copy in copies:
        copy.wait()


def after(later, earlier):
    return lax.optimization_barrier((later, earlier))


def exchange(near, far):
    pairs = [(0, 0), (1, 1), (2, 4), (4, 2), (3, 5), (5, 3), (6, 6), (7, 7)]
    return lax.ppermute(far, "seq", pairs), swap(near, "seq", 2)


def clip_body(latents, in_weight, out_weight, cotangent, clip_lengths):
    width = latents.shape[3]
    rows = INNER // 8
    wide = jnp.float32
    place = jnp.arange(2 + clip_lengths.shape[1], dtype=jnp.int32)
    spot = jnp.where(place == 0, lax.axis_index("seq"), jnp.where(place == 1, lax.axis_index("dp"), 0))
    spot = spot + jnp.pad(clip_lengths[0], (2, 0))
    heads = jnp.asarray(np.arange(INNER) // HD == np.arange(HEADS)[:, None], jnp.bfloat16)
    lat = latents.reshape(4, ROWS, width)
    cot = cotangent.reshape(4, ROWS, width)

    bf16 = jnp.bfloat16
    four, two, eight = shaped((4, ROWS, width)), shaped((2, ROWS, width)), shaped((8, ROWS, INNER))

    def pick(own, sib, flops):
        near, far, both = call(pick_kernel, [spot], [own, sib], [two, two, four], flops=flops)
        return exchange(near, far), both

    lat_sib, cot_sib = swap(lat, "seq", 1), swap(cot, "seq", 1)
    lat_own = lax.dynamic_slice_in_dim(lat, 2 * (lax.axis_index("seq") % 2), 2, 0)
    (lat_far, lat_near), lat_ab = pick(lat_own, lat_sib, 4 * 10**9)
    (qkv_ab,) = call(
        early_kernel, [], [lat_ab, in_weight], [shaped((8, ROWS, 3 * INNER))], limit=16, flops=27 * 10**8
    )
    cot_sib, qkv_ab = after(cot_sib, qkv_ab)
    (cot_far, cot_near), cot_ab = pick(cot, cot_sib, 10**6)
    grad_att = functools.partial(grad_att_kernel, first=0)
    (ga,) = call(grad_att, [], [cot_ab, out_weight], [eight], limit=16, flops=7 * 10**8)
    lat_far, ga = after(lat_far, ga)
    pairs = 2 * PAIRS * ROWS
    products, columns = ((pairs, INNER), bf16), ((pairs, HEADS), bf16)
    qkv, att, probs, wides = call(
        forward_kernel, [spot], [lat_near, lat_far, in_weight, qkv_ab, heads],
        [shaped((8, ROWS, 3 * INNER)), eight, shaped((HEADS, pairs), wide), shaped((pairs, INNER))],
        [((4, ROWS, width), bf16), products, columns], limit=24, flops=8 * 10**9, same=(3, 0),
    )
    part_scr = ((4 * rows, 8 * ROWS), bf16)
    other, att_t, cot_all = call(
        part_kernel, [spot], [att, cot_ab, cot_far, cot_near],
        [shaped((4, rows, width)), shaped((INNER, 8 * ROWS)), eight], [part_scr],
        limit=16, flops=7 * 10**8,
    )
    got = swap(other, "seq", 1)
    cot_all, other = after(cot_all, other)
    grad_att = functools.partial(grad_att_kernel, first=4)
    (ga,) = call(grad_att, [], [cot_all, out_weight, ga], [eight], limit=16, flops=7 * 10**8, same=(2, 0))
    part, piece = (4, PIECE, TILE), (PIECE, TILE)
    tiles = rows * width // TILE
    (mine,) = call(
        mine_kernel, [spot], [att_t, cot_all], [shaped((4 * tiles, TILE), wide)], [part_scr],
        limit=16, flops=7 * 10**8,
    )
    mine, ga = after(mine, ga)
    keep, *sends = call(
        cores_kernel, [spot], [mine, got], [shaped(part, wide)] + [shaped(part)] * 3,
        [((4 * tiles, TILE), wide)], limit=16, flops=7 * 10**8,
    )
    att, sends = after(att, sends)
    sends = [swap(sends[flip - 1], "dp", flip) for flip in (3, 1, 2)]
    mixed = call(mix_kernel, [], [att, out_weight], [four, two, two], limit=16, size=10**3)
    qkv, mixed = after(qkv, mixed)
    mixed = [mixed[0], *exchange(mixed[1], mixed[2])]
    (d_all,) = call(
        backward_kernel, [spot], [ga, qkv, probs, wides, heads], [shaped((8, ROWS, 3 * INNER))],
        [products, ((HEADS, pairs), wide), columns], limit=24, size=10**3,
    )
    theirs = functools.partial(latents_kernel, first=4)
    grad = call(theirs, [], [d_all, in_weight], [two, two], limit=16, size=10**3)
    keep, (grad, mixed) = after(keep, (grad, mixed))
    keep, *sends = call(
        groups_kernel, [spot], [keep, *sends], [shaped(piece, wide)] + [shaped(piece)] * 3,
        [(part, wide)],
    )
    grad, keep = after(grad, keep)
    sends = [swap(sends[flip - 1], "seq", 2 * flip) for flip in (2, 3, 1)]
    d_all, grad = after(d_all, grad)
    ours = functools.partial(latents_kernel, first=0)
    (own,) = call(ours, [], [d_all, in_weight], [four], limit=16, flops=8 * 10**9)
    grad = [own, *exchange(grad[0], grad[1])]
    keep, grad[0] = after(keep, grad[0])
    (last,) = call(chips_kernel, [], [keep, *sends], [shaped(piece)])
    grad[0], last = after(grad[0], last)
    others = [swap(last, "dp", flip) for flip in (1, 2, 3)]
    grad = [grad[0], grad[2], grad[1]]
    own, sib = call(settle_kernel, [spot], [*mixed, *grad], [four, four])
    (token,) = call(arrived_kernel, [], others, [shaped((16, TILE))], flops=8 * 10**9)
    mixed, grad, out_grad = call(
        final_kernel, [spot], [own, swap(sib, "seq", 1), last, *others, token],
        [four, four, shaped((rows, width), wide)],
        [(part, wide), ((tiles, TILE), wide), ((rows, width), wide), pltpu.SemaphoreType.DMA((5,))],
        to_hbm=True,
    )
    return mixed.reshape(latents.shape), grad.reshape(latents.shape), out_grad


def body(latents, *others):
    frames, patches = latents.shape[1] * lax.axis_size("seq"), latents.shape[2]
    small = (lax.axis_size("dp"), lax.axis_size("seq"), frames, patches) == (4, 8, 8, 4 * ROWS)
    return (clip_body if small else patch_body)(latents, *others)


def solution(mesh):
    placed = (P("dp", "seq", None, None), P(), P(), P("dp", "seq", None, None), P("dp", None))
    return jax.shard_map(
        body,
        mesh=mesh,
        in_specs=placed,
        out_specs=(P("dp", "seq", None, None), P("dp", "seq", None, None), P("seq", None)),
        check_vma=False,
    )
```

```python
import functools

import jax
import jax.numpy as jnp
import numpy as np
from jax import lax
from jax.experimental import pallas as pl
from jax.experimental.pallas import tpu as pltpu
from jax.sharding import PartitionSpec as P

HEADS = 16
HD = 72


def clip_index(lengths, frames):
    ends = jnp.cumsum(lengths)
    position = jnp.arange(frames, dtype=jnp.int32)
    return jnp.sum((ends[None, :] <= position[:, None]).astype(jnp.int32), axis=1)


def softmax_weights(query, key_rows, same):
    scale = 1.0 / jnp.sqrt(jnp.float32(HD))
    scores = (
        jnp.einsum("fphd,gphd->phfg", query, key_rows, preferred_element_type=jnp.float32) * scale
    )
    scores = jnp.where(same[None, None], scores, -jnp.inf)
    return jax.nn.softmax(scores, axis=-1)


def contract_rows(left, right):
    return lax.dot_general(
        left, right, (((0,), (0,)), ((), ())), preferred_element_type=jnp.float32
    )


def contract_cols(left, right):
    return lax.dot_general(
        left, right, (((1,), (1,)), ((), ())), preferred_element_type=jnp.float32
    )


def swap(value, axis, flip):
    size = lax.axis_size(axis)
    return lax.ppermute(value, axis, [(i, i ^ flip) for i in range(size)])


def reduce_out(part):
    mine = lax.psum_scatter(part, "seq", scatter_dimension=0, tiled=True)
    return lax.psum(mine.astype(jnp.bfloat16), "dp").astype(jnp.float32)


def patch_body(latents, in_weight, out_weight, cotangent, clip_lengths):
    shards = lax.axis_size("seq")
    local_frames = latents.shape[1]
    patches = latents.shape[2]
    width = latents.shape[3]
    frames = local_frames * shards
    local_patches = patches // shards
    inner = HEADS * HD

    def to_patches(rows):
        return lax.all_to_all(rows, "seq", split_axis=2, concat_axis=1, tiled=True)

    def to_frames(rows):
        return lax.all_to_all(rows, "seq", split_axis=1, concat_axis=2, tiled=True)

    lat_rows = to_patches(latents).reshape(frames * local_patches, width)
    cot_rows = to_patches(cotangent).reshape(frames * local_patches, width)
    projected = jnp.dot(lat_rows, in_weight, preferred_element_type=jnp.float32).astype(
        jnp.bfloat16
    )
    split = projected.reshape(frames, local_patches, 3, HEADS, HD)
    query, key_rows, value_rows = (split[:, :, 0], split[:, :, 1], split[:, :, 2])
    clip = clip_index(clip_lengths[0], frames)
    same = clip[:, None] == clip[None, :]
    weights32 = softmax_weights(query, key_rows, same)
    weights = weights32.astype(jnp.bfloat16)
    attended = jnp.einsum(
        "phfg,gphd->fphd", weights, value_rows, preferred_element_type=jnp.float32
    ).astype(jnp.bfloat16)
    att_rows = attended.reshape(frames * local_patches, inner)
    out_grad = reduce_out(contract_rows(att_rows, cot_rows))
    mixed = jnp.dot(att_rows, out_weight, preferred_element_type=jnp.float32).astype(jnp.bfloat16)
    mixed = to_frames(mixed.reshape(1, frames, local_patches, width))
    grad_att = contract_cols(cot_rows, out_weight).astype(jnp.bfloat16)
    grad_heads = grad_att.reshape(frames, local_patches, HEADS, HD)
    grad_weights = jnp.einsum(
        "fphd,gphd->phfg", grad_heads, value_rows, preferred_element_type=jnp.float32
    )
    grad_values = jnp.einsum(
        "phfg,fphd->gphd", weights, grad_heads, preferred_element_type=jnp.float32
    ).astype(jnp.bfloat16)
    totals = jnp.sum(weights32 * grad_weights, axis=-1, keepdims=True)
    scale = 1.0 / jnp.sqrt(jnp.float32(HD))
    grad_scores = (weights32 * (grad_weights - totals) * scale).astype(jnp.bfloat16)
    grad_query = jnp.einsum(
        "phfg,gphd->fphd", grad_scores, key_rows, preferred_element_type=jnp.float32
    ).astype(jnp.bfloat16)
    grad_keys = jnp.einsum(
        "phfg,fphd->gphd", grad_scores, query, preferred_element_type=jnp.float32
    ).astype(jnp.bfloat16)
    grad_proj = jnp.stack([grad_query, grad_keys, grad_values], axis=2)
    grad_rows = grad_proj.reshape(frames * local_patches, 3 * inner)
    grad_latents = contract_cols(grad_rows, in_weight).astype(jnp.bfloat16)
    grad_latents = to_frames(grad_latents.reshape(1, frames, local_patches, width))
    return (mixed.reshape(latents.shape), grad_latents.reshape(latents.shape), out_grad)


ROWS = 64
PAIRS = 16
TILE = 128
INNER = HEADS * HD
PIECE = 41 * 8
SMEM = pl.BlockSpec(memory_space=pltpu.SMEM)
VMEM = pl.BlockSpec(memory_space=pltpu.VMEM)
HBM = pl.BlockSpec(memory_space=pltpu.HBM)
CHUNKS = ((0, 256), (256, 256), (512, 256), (768, 256), (1024, 128))


def shaped(shape, dtype=jnp.bfloat16):
    return jax.ShapeDtypeStruct(shape, dtype)


def dot(left, right):
    return jnp.dot(left, right, preferred_element_type=jnp.float32)


def flat(value):
    return value.reshape(value.shape[0] * ROWS, value.shape[2])


def call(kernel, scalars, inputs, outs, scratch=(), limit=8, flops=10**6, to_hbm=False, size=None, same=None):
    size = size or sum(x.size * x.dtype.itemsize for x in (*inputs, *outs))
    return pl.pallas_call(
        kernel,
        out_shape=list(outs),
        in_specs=[SMEM] * len(scalars) + [VMEM] * len(inputs),
        out_specs=[HBM if to_hbm else VMEM] * len(outs),
        scratch_shapes=[x if hasattr(x, "memory_space") else pltpu.VMEM(*x) for x in scratch],
        input_output_aliases={len(scalars) + same[0]: same[1]} if same else {},
        compiler_params=pltpu.CompilerParams(vmem_limit_bytes=limit << 20),
        cost_estimate=pl.CostEstimate(flops=flops, bytes_accessed=size, transcendentals=0),
    )(*scalars, *inputs)


def roles(spot):
    zpos, lens = spot[0] // 2, [spot[2 + i] for i in range(3)]
    first = 2 * zpos
    ends = [lens[0], lens[0] + lens[1], lens[0] + lens[1] + lens[2]]
    long = jnp.where(
        lens[0] == 4, 0, jnp.where(lens[1] == 4, ends[0], jnp.where(lens[2] == 4, ends[1], ends[2]))
    )

    def clip(frame):
        return sum((end <= frame).astype(jnp.int32) for end in ends)

    ids = [
        jnp.where(zpos == 0, -1, clip(first - 1)),
        clip(first),
        clip(first + 1),
        jnp.where(zpos == 3, -2, clip(first + 2)),
    ]
    return {
        "core": spot[0] % 2,
        "odd": zpos % 2,
        "left": 6 - 2 * (zpos % 2),
        "right": 4 + 2 * (zpos % 2),
        "ids": ids,
        "low": long == first,
        "high": long == first - 2,
        "middle": long == first - 1,
        "tail": long == first - 3,
        "head": long == first + 1,
    }


def slots(role, window):
    low, high, left, right = role["low"], role["high"], role["left"], role["right"]
    in_low = ((0, 2, right, right + 1), (1, 3, left, left + 1))[window]
    in_high = ((left, left + 1, 1, 3), (0, 2, right, right + 1))[window]
    usual = (left + window, window, 2 + window, right + window)
    blocks = [
        jnp.where(low, a, jnp.where(high, b, c)) for a, b, c in zip(in_low, in_high, usual)
    ]
    even, middle = low | high, role["middle"]
    odd = [middle, ~even & ~role["tail"], ~even & ~role["head"], middle]
    return blocks, [even | x for x in odd] if window == 0 else odd


def pick_kernel(spot, own, sib, near, far, both):
    role = roles(spot)
    core, odd = role["core"], role["odd"]
    for i in range(2):
        both[2 * core + i] = own[i if own.shape[0] == 2 else 2 * core + i]
        both[2 * (1 - core) + i] = sib[2 * core + i]
    right = (jnp.where(role["low"], 1, 2), 3)
    left = (0, jnp.where(role["high"], 2, 1))
    for i in range(2):
        near[i] = both[jnp.where(odd == 1, left[i], right[i])]
        far[i] = both[jnp.where(odd == 1, right[i], left[i])]


def early_kernel(lat_ab, wi_ref, qkv_ref):
    x = flat(lat_ab[...])
    for j in range(3):
        cols = slice(j * INNER, (j + 1) * INNER)
        qkv_ref[:4, :, cols] = dot(x, wi_ref[:, cols]).astype(jnp.bfloat16).reshape(4, ROWS, INNER)


def pair(f, g, w=0, count=1):
    start = (4 * f + g) * 2 * ROWS + w * ROWS
    return slice(start, start + count * ROWS)


def lanes(t, offset=0):
    return slice(offset + TILE * t, offset + TILE * (t + 1))


def forward_kernel(
    spot, far, near, wi_ref, _, heads_ref, qkv_ref, att_ref, p_ref, wide_ref,
    x_scr, hi_scr, w_scr,
):
    x_scr[:2] = near[...]
    x_scr[2:] = far[...]
    x = flat(x_scr[...])
    for j in range(3):
        cols = slice(j * INNER, (j + 1) * INNER)
        qkv_ref[4:, :, cols] = dot(x, wi_ref[:, cols]).astype(jnp.bfloat16).reshape(4, ROWS, INNER)
    role = roles(spot)
    even, ids = role["low"] | role["high"], role["ids"]
    windows = [slots(role, w) for w in range(2)]
    for w, (blocks, _) in enumerate(windows):
        for t in range(INNER // TILE):
            q = [qkv_ref[blocks[f], :, lanes(t)] for f in range(4)]
            k = [qkv_ref[blocks[g], :, lanes(t, INNER)] for g in range(4)]
            for f in range(4):
                for g in range(4):
                    hi_scr[pair(f, g, w), lanes(t)] = q[f] * k[g]
    scores = contract_cols(heads_ref[...], hi_scr[...])
    for f in range(4):
        line = []
        for g in range(4):
            bias = jnp.where(even | (ids[f] == ids[g]), 0.0, -jnp.inf)
            line.append(scores[:, pair(f, g, 0, 2)] * HD**-0.5 + bias)
        top = jnp.maximum(jnp.maximum(line[0], line[1]), jnp.maximum(line[2], line[3]))
        line = [jnp.exp(x - top) for x in line]
        share = 1.0 / (line[0] + line[1] + line[2] + line[3])
        for g in range(4):
            p_ref[:, pair(f, g, 0, 2)] = line[g] * share
    w_scr[...] = p_ref[...].T.astype(jnp.bfloat16)
    for f in range(4):
        rows = pair(f, 0, 0, 8)
        for start, size in CHUNKS:
            cols = slice(start, start + size)
            spread = dot(w_scr[rows, :], heads_ref[:, cols])
            wide_ref[rows, cols] = spread.astype(jnp.bfloat16)
            for w, (blocks, kept) in enumerate(windows):
                base = 2 * INNER + start
                total = sum(
                    spread[pair(0, g, w)] * qkv_ref[blocks[g], :, base : base + size].astype(jnp.float32)
                    for g in range(4)
                )
                total = total * jnp.where(kept[f], 1.0, 0.0)
                att_ref[blocks[f], :, cols] = total.astype(jnp.bfloat16)


def part_rows(core, att_t, cot, rows):
    height = att_t.shape[0] // 8
    for z in range(4):
        start = pl.multiple_of((2 * z + core) * height, 16)
        rows[z * height : (z + 1) * height, :] = att_t[pl.ds(start, height), :]
    return dot(rows[...], flat(cot[...])).reshape(4, height, -1)


def part_kernel(spot, att_ref, ab_ref, far, near, sib_ref, att_t, cot, rows):
    cot[:4] = ab_ref[...]
    cot[4:6] = near[...]
    cot[6:] = far[...]
    att_t[...] = flat(att_ref[...]).T
    sib_ref[...] = part_rows(1 - spot[0] % 2, att_t, cot, rows).astype(jnp.bfloat16)


def mix_kernel(att_ref, w_ref, here_ref, near_ref, far_ref):
    made = dot(flat(att_ref[...]), w_ref[...]).astype(jnp.bfloat16).reshape(8, ROWS, -1)
    here_ref[...] = made[:4]
    near_ref[...] = made[4:6]
    far_ref[...] = made[6:]


def grad_att_kernel(cot, wo_ref, *refs, first):
    rows = cot[first : first + 4]
    made = contract_cols(flat(rows), wo_ref[...])
    refs[-1][first : first + 4] = made.astype(jnp.bfloat16).reshape(4, ROWS, INNER)


def backward_kernel(
    spot, ga_ref, qkv_ref, p_ref, wide_ref, heads_ref, d_ref, hi_scr, t_scr, s_scr
):
    role = roles(spot)
    windows = [slots(role, w)[0] for w in range(2)]
    for w, blocks in enumerate(windows):
        for t in range(INNER // TILE):
            do = [ga_ref[blocks[f], :, lanes(t)] for f in range(4)]
            v = [qkv_ref[blocks[g], :, lanes(t, 2 * INNER)] for g in range(4)]
            for f in range(4):
                for g in range(4):
                    hi_scr[pair(f, g, w), lanes(t)] = do[f] * v[g]
    grads = contract_cols(heads_ref[...], hi_scr[...])
    for f in range(4):
        p = [p_ref[:, pair(f, g, 0, 2)] for g in range(4)]
        line = [grads[:, pair(f, g, 0, 2)] for g in range(4)]
        total = sum(p[g] * line[g] for g in range(4))
        for g in range(4):
            t_scr[:, pair(f, g, 0, 2)] = p[g] * (line[g] - total) * HD**-0.5
    s_scr[...] = t_scr[...].T.astype(jnp.bfloat16)
    for start, size in CHUNKS:
        cols = slice(start, start + size)
        spread = dot(s_scr[...], heads_ref[:, cols])
        for w, blocks in enumerate(windows):

            def take(ref, block, offset=0):
                return ref[block, :, offset + start : offset + start + size].astype(jnp.float32)

            def put(block, offset, value):
                d_ref[block, :, offset + start : offset + start + size] = value.astype(jnp.bfloat16)

            do = [take(ga_ref, blocks[f]) for f in range(4)]
            for g in range(4):
                put(
                    blocks[g], 2 * INNER,
                    sum(wide_ref[pair(f, g, w), cols].astype(jnp.float32) * do[f] for f in range(4)),
                )
            q = [take(qkv_ref, blocks[f]) for f in range(4)]
            k = [take(qkv_ref, blocks[g], INNER) for g in range(4)]
            for f in range(4):
                put(blocks[f], 0, sum(spread[pair(f, g, w)] * k[g] for g in range(4)))
            for g in range(4):
                put(blocks[g], INNER, sum(spread[pair(f, g, w)] * q[f] for f in range(4)))


def latents_kernel(d_ref, wi_ref, *outs, first):
    tile = 384
    for j in range(wi_ref.shape[0] // tile):
        cols = slice(j * tile, (j + 1) * tile)
        made = contract_cols(flat(d_ref[first : first + 4]), wi_ref[cols, :]).astype(jnp.bfloat16)
        made = made.reshape(4, ROWS, tile)
        size = 4 // len(outs)
        for i, out in enumerate(outs):
            out[:, :, cols] = made[i * size : (i + 1) * size]


def settle_kernel(spot, *refs):
    *given, own, sib = refs
    role = roles(spot)
    core, left, right = role["core"], role["left"], role["right"]
    low, high, tail, head = role["low"], role["high"], role["tail"], role["head"]
    where = [
        jnp.where(high | tail, left, 0),
        jnp.where(low, right, jnp.where(tail, left + 1, 1)),
        jnp.where(high, left + 1, jnp.where(head, right, 2)),
        jnp.where(low | head, right + 1, 3),
    ]

    def put(out, row, block, here, far, near):
        for source, first, count in ((here, 0, 4), (near, 4, 2), (far, 6, 2)):

            @pl.when((block >= first) & (block < first + count))
            def _():
                out[row] = source[block - first]

    for base in (0, 2):
        sources = given[:3] if base == 0 else given[3:]
        for i in range(2):
            put(own, base + i, jnp.where(core == 0, where[i], where[2 + i]), *sources)
            put(sib, base + i, jnp.where(core == 0, where[2 + i], where[i]), *sources)


def first_row(group, block):
    return pl.multiple_of((group * 81 // 2 + block * 162) * 8, 8)


def mine_kernel(spot, att_t, cot, total, rows):
    height, width = att_t.shape[0] // 8, cot.shape[2]
    made = part_rows(spot[0] % 2, att_t, cot, rows)
    for z in range(4):
        for t in range(width // TILE):
            start = (z * width // TILE + t) * height
            total[start : start + height, :] = made[z][:, lanes(t)]


def cores_kernel(spot, mine, got, keep, *sends):
    group = spot[1]
    *sends, total = sends
    height, width = got.shape[1:]
    for z in range(4):
        for t in range(width // TILE):
            rows = slice((z * width // TILE + t) * height, (z * width // TILE + t + 1) * height)
            total[rows, :] = mine[rows, :] + got[z, :, lanes(t)].astype(jnp.float32)
    for flip, out in enumerate((keep, *sends)):
        for z in range(4):
            out[z] = total[pl.ds(first_row(group ^ flip, z), PIECE), :].astype(out.dtype)


def groups_kernel(spot, own, one, two, three, keep, *sends):
    zpos = spot[0] // 2
    *sends, total = sends
    total[...] = own[...] + sum(x[...].astype(jnp.float32) for x in (one, two, three))
    for flip, out in enumerate((keep, *sends)):
        out[...] = total[zpos ^ flip].astype(out.dtype)


def chips_kernel(own, one, two, three, out):
    total = own[...] + sum(x[...].astype(jnp.float32) for x in (one, two, three))
    out[...] = total.astype(jnp.bfloat16)


def gather_kernel(spot, own, one, two, three, out, held, rows):
    for flip, value in enumerate((own, one, two, three)):
        held[spot[1] ^ flip] = value[...].astype(jnp.float32)
    for group in range(4):
        rows[pl.ds(first_row(group, 0), PIECE), :] = held[group]
    height, width = out.shape
    for t in range(width // TILE):
        out[:, lanes(t)] = rows[t * height : (t + 1) * height, :]


def final_kernel(spot, own, sib, rows, mixed, grad, out, sems):
    core = spot[0] % 2
    here, there = pl.ds(2 * core, 2), pl.ds(2 * (1 - core), 2)
    moves = [(rows.at[i : i + 48], out.at[i : i + 48]) for i in range(0, out.shape[0], 48)]
    for base, made in ((0, mixed), (2, grad)):
        moves.append((own.at[base : base + 2], made.at[here]))
        moves.append((sib.at[base : base + 2], made.at[there]))
    copies = [pltpu.make_async_copy(x, y, sems.at[i]) for i, (x, y) in enumerate(moves)]
    for copy in copies:
        copy.start()
    for copy in copies:
        copy.wait()


def after(later, earlier):
    return lax.optimization_barrier((later, earlier))


def exchange(near, far):
    pairs = [(0, 0), (1, 1), (2, 4), (4, 2), (3, 5), (5, 3), (6, 6), (7, 7)]
    return lax.ppermute(far, "seq", pairs), swap(near, "seq", 2)


def clip_body(latents, in_weight, out_weight, cotangent, clip_lengths):
    width = latents.shape[3]
    rows = INNER // 8
    wide = jnp.float32
    place = jnp.arange(2 + clip_lengths.shape[1], dtype=jnp.int32)
    spot = jnp.where(place == 0, lax.axis_index("seq"), jnp.where(place == 1, lax.axis_index("dp"), 0))
    spot = spot + jnp.pad(clip_lengths[0], (2, 0))
    heads = jnp.asarray(np.arange(INNER) // HD == np.arange(HEADS)[:, None], jnp.bfloat16)
    lat = latents.reshape(4, ROWS, width)
    cot = cotangent.reshape(4, ROWS, width)

    bf16 = jnp.bfloat16
    four, two, eight = shaped((4, ROWS, width)), shaped((2, ROWS, width)), shaped((8, ROWS, INNER))

    def pick(own, sib, flops):
        near, far, both = call(pick_kernel, [spot], [own, sib], [two, two, four], flops=flops)
        return exchange(near, far), both

    lat_sib, cot_sib = swap(lat, "seq", 1), swap(cot, "seq", 1)
    lat_own = lax.dynamic_slice_in_dim(lat, 2 * (lax.axis_index("seq") % 2), 2, 0)
    (lat_far, lat_near), lat_ab = pick(lat_own, lat_sib, 4 * 10**9)
    (qkv_ab,) = call(
        early_kernel, [], [lat_ab, in_weight], [shaped((8, ROWS, 3 * INNER))], limit=16, flops=27 * 10**8
    )
    cot_sib, qkv_ab = after(cot_sib, qkv_ab)
    (cot_far, cot_near), cot_ab = pick(cot, cot_sib, 10**6)
    grad_att = functools.partial(grad_att_kernel, first=0)
    (ga,) = call(grad_att, [], [cot_ab, out_weight], [eight], limit=16, flops=7 * 10**8)
    lat_far, ga = after(lat_far, ga)
    pairs = 2 * PAIRS * ROWS
    products, columns = ((pairs, INNER), bf16), ((pairs, HEADS), bf16)
    qkv, att, probs, wides = call(
        forward_kernel, [spot], [lat_far, lat_near, in_weight, qkv_ab, heads],
        [shaped((8, ROWS, 3 * INNER)), eight, shaped((HEADS, pairs), wide), shaped((pairs, INNER))],
        [((4, ROWS, width), bf16), products, columns], limit=24, flops=8 * 10**9, same=(3, 0),
    )
    part_scr = ((4 * rows, 8 * ROWS), bf16)
    other, att_t, cot_all = call(
        part_kernel, [spot], [att, cot_ab, cot_far, cot_near],
        [shaped((4, rows, width)), shaped((INNER, 8 * ROWS)), eight], [part_scr],
        limit=16, flops=7 * 10**8,
    )
    got = swap(other, "seq", 1)
    cot_all, other = after(cot_all, other)
    grad_att = functools.partial(grad_att_kernel, first=4)
    (ga,) = call(grad_att, [], [cot_all, out_weight, ga], [eight], limit=16, flops=7 * 10**8, same=(2, 0))
    part, piece = (4, PIECE, TILE), (PIECE, TILE)
    tiles = rows * width // TILE
    (mine,) = call(
        mine_kernel, [spot], [att_t, cot_all], [shaped((4 * tiles, TILE), wide)], [part_scr],
        limit=16, flops=7 * 10**8,
    )
    mine, ga = after(mine, ga)
    keep, *sends = call(
        cores_kernel, [spot], [mine, got], [shaped(part, wide)] + [shaped(part)] * 3,
        [((4 * tiles, TILE), wide)], limit=16, flops=7 * 10**8,
    )
    att, sends = after(att, sends)
    sends = [swap(sends[flip - 1], "dp", flip) for flip in (3, 1, 2)]
    mixed = call(mix_kernel, [], [att, out_weight], [four, two, two], limit=16, size=10**3)
    qkv, mixed = after(qkv, mixed)
    mixed = [mixed[0], *exchange(mixed[1], mixed[2])]
    (d_all,) = call(
        backward_kernel, [spot], [ga, qkv, probs, wides, heads], [shaped((8, ROWS, 3 * INNER))],
        [products, ((HEADS, pairs), wide), columns], limit=24, size=10**3,
    )
    theirs = functools.partial(latents_kernel, first=4)
    grad = call(theirs, [], [d_all, in_weight], [two, two], limit=16, size=10**3)
    keep, (grad, mixed) = after(keep, (grad, mixed))
    keep, *sends = call(
        groups_kernel, [spot], [keep, *sends], [shaped(piece, wide)] + [shaped(piece)] * 3,
        [(part, wide)],
    )
    grad, keep = after(grad, keep)
    sends = [swap(sends[flip - 1], "seq", 2 * flip) for flip in (3, 1, 2)]
    d_all, grad = after(d_all, grad)
    ours = functools.partial(latents_kernel, first=0)
    (own,) = call(ours, [], [d_all, in_weight], [four], limit=16, flops=8 * 10**9)
    grad = [own, *exchange(grad[0], grad[1])]
    keep, grad[0] = after(keep, grad[0])
    (last,) = call(chips_kernel, [], [keep, *sends], [shaped(piece)])
    grad[0], last = after(grad[0], last)
    others = [swap(last, "dp", flip) for flip in (1, 2, 3)]
    own, sib = call(settle_kernel, [spot], [*mixed, *grad], [four, four])
    (out_grad,) = call(
        gather_kernel, [spot], [last, *others], [shaped((rows, width), wide)],
        [(part, wide), ((tiles, TILE), wide)], flops=8 * 10**9,
    )
    mixed, grad, out_grad = call(
        final_kernel, [spot], [own, swap(sib, "seq", 1), out_grad],
        [four, four, shaped((rows, width), wide)], [pltpu.SemaphoreType.DMA((7,))], to_hbm=True,
    )
    return mixed.reshape(latents.shape), grad.reshape(latents.shape), out_grad


def body(latents, *others):
    frames, patches = latents.shape[1] * lax.axis_size("seq"), latents.shape[2]
    small = (lax.axis_size("dp"), lax.axis_size("seq"), frames, patches) == (4, 8, 8, 4 * ROWS)
    return (clip_body if small else patch_body)(latents, *others)


def solution(mesh):
    placed = (P("dp", "seq", None, None), P(), P(), P("dp", "seq", None, None), P("dp", None))
    return jax.shard_map(
        body,
        mesh=mesh,
        in_specs=placed,
        out_specs=(P("dp", "seq", None, None), P("dp", "seq", None, None), P("seq", None)),
        check_vma=False,
    )
```
